128 devices in a mesh: gy: 8 (over x_lo, y), gx: 16 (over z, x_hi, core).
Axes of the slice: x: 4 (x_hi: 2, x_lo: 2; x = x_hi * 2 + x_lo), y: 4, z: 4, core: 2. Of those that a mesh axis runs over, the one named last changes fastest.
Arguments:
- coded: bfloat16 [512, 1536, 256], P('gy', 'gx'), may hold values from -6 to 6
- tile_scales: float32 [64, 192, 256], P('gy', 'gx'), may hold values from 0.25 to 4
- expand_weight: bfloat16 [256, 1024], replicated, may hold values from -0.375 to 0.375
- expand_bias: float32 [1024], replicated, may hold values from -3 to 3
- depth_kernel: float32 [9, 1024], replicated, may hold values from -2 to 2
- depth_bias: float32 [1024], replicated, may hold values from -3 to 3
- project_weight: bfloat16 [1024, 256], replicated, may hold values from -0.1875 to 0.1875
- project_bias: float32 [256], replicated, may hold values from -3 to 3
- query_weight: bfloat16 [256, 256], replicated, may hold values from -2 to 2
- key_weight: bfloat16 [256, 256], replicated, may hold values from -2 to 2
- value_weight: bfloat16 [256, 256], replicated, may hold values from -0.375 to 0.375
- out_weight: bfloat16 [256, 256], replicated, may hold values from -0.375 to 0.375
Outputs:
- block_out: bfloat16 [512, 1536, 256], P('gy', 'gx')
The draws below stay inside these ranges and needn't reach their ends.
All inputs are finite; a program needn't handle non-finite values.
Results may differ from the reference program's by a relative error of at most 0.015.
Values may be sent and summed in bfloat16 or wider, within the bound.
No kernel may reach another device: no remote copies, remote signals or barrier semaphores. Data moves between devices by JAX's collectives and lax.ppermute only.
A program may use at most 192 MiB of HBM per device.

```python
import math
import jax
import jax.numpy as jnp
from jax import lax

C = 256
FF = 1024
HEAD_DIM = 32
GRID = 8
TILE = 8
ROWS = 512
COLS = 1536


def shared_matrix(key):
    return jnp.clip(jax.random.normal(key, (C, C), jnp.float32), -4.0, 4.0) * C ** (-0.5)


def draw_query_weight(key, part):
    key = jax.random.fold_in(key, 11)
    own = shared_matrix(key)
    return own.astype(jnp.bfloat16)


def draw_key_weight(key, part):
    key = jax.random.fold_in(key, 12)
    own = shared_matrix(key)
    return own.astype(jnp.bfloat16)


def shard_levels(stream_key, extent, cuts, low, top_value):
    factor_of, own = 1.0, jax.random.fold_in(stream_key, 6)
    for axis_at, blocks in cuts:
        draws = jnp.exp(jax.random.uniform(jax.random.fold_in(own, axis_at), (blocks,), jnp.float32, low / len(cuts), top_value / len(cuts)))
        factor_of = factor_of * jnp.repeat(draws, extent[axis_at] // blocks).reshape([-1 if axis == axis_at else 1 for axis in range(len(extent))])
    return factor_of


def gaussian(rng, shape, scale, most, shards=(), held_as=jnp.bfloat16):
    entries = jax.random.normal(rng, shape, jnp.float32) * scale
    if len(shards) > 0:
        entries = shard_levels(rng, shape, shards, -0.22, 0.18) * entries
    return jnp.clip(entries, min=-most, max=most).astype(held_as)


def setup_inputs(seed: int = 0) -> dict:
    arg_keys = jax.random.split(jax.random.key(seed), 13)
    return {
        "coded": gaussian(arg_keys[0], (ROWS, COLS, C), 1.0, 6.0, ((0, 8), (1, 16))),
        "tile_scales": jnp.clip(jnp.exp(math.log(4.0) - 2.7725887 * jax.random.uniform(arg_keys[1], (ROWS // TILE, COLS // TILE, C), jnp.float32) ** shard_levels(arg_keys[1], (ROWS // TILE, COLS // TILE, C), ((0, 8), (1, 16)), -0.2, 0.2)), 0.25, 4.0),
        "expand_weight": gaussian(arg_keys[2], (C, FF), C ** -0.5, 0.375),
        "expand_bias": gaussian(arg_keys[3], (FF,), 0.5, 3.0, (), jnp.float32),
        "depth_kernel": gaussian(arg_keys[4], (9, FF), 0.33, 2.0, (), jnp.float32),
        "depth_bias": gaussian(arg_keys[5], (FF,), 0.5, 3.0, (), jnp.float32),
        "project_weight": gaussian(arg_keys[6], (FF, C), FF ** -0.5, 0.1875),
        "project_bias": gaussian(arg_keys[7], (C,), 0.5, 3.0, (), jnp.float32),
        "query_weight": draw_query_weight(jax.random.fold_in(arg_keys[12], 71), 0),
        "key_weight": draw_key_weight(jax.random.fold_in(arg_keys[12], 71), 0),
        "value_weight": gaussian(arg_keys[10], (C, C), C ** -0.5, 0.375),
        "out_weight": gaussian(arg_keys[11], (C, C), C ** -0.5, 0.375),
    }


def gelu(v):
    return jax.nn.gelu(v, approximate=True)

def attend(groups, query_weight, key_weight, value_weight, out_weight):
    count, cells, chans = groups.shape
    values_f = groups.astype(jnp.float32)
    center = lax.optimization_barrier(jnp.mean(values_f, axis=-1, keepdims=True))
    spread = lax.optimization_barrier(jnp.mean((values_f - center) ** 2, axis=-1, keepdims=True))
    normed = ((values_f - center) * lax.rsqrt(spread + 1e-05)).astype(jnp.bfloat16).reshape(-1, chans)
    heads = chans // HEAD_DIM
    queries = jnp.dot(normed, query_weight, preferred_element_type=jnp.float32).astype(jnp.bfloat16)
    keys = jnp.dot(normed, key_weight, preferred_element_type=jnp.float32).astype(jnp.bfloat16)
    values = jnp.dot(normed, value_weight, preferred_element_type=jnp.float32).astype(jnp.bfloat16)
    queries = queries.reshape(count, cells, heads, HEAD_DIM)
    keys = keys.reshape(count, cells, heads, HEAD_DIM)
    values = values.reshape(count, cells, heads, HEAD_DIM)
    scores = jnp.einsum('bqhd,bkhd->bhqk', queries, keys, preferred_element_type=jnp.float32)
    scores = scores / jnp.sqrt(jnp.float32(HEAD_DIM))
    weights = jax.nn.softmax(scores, axis=-1).astype(jnp.bfloat16)
    attended = jnp.einsum('bhqk,bkhd->bqhd', weights, values, preferred_element_type=jnp.float32)
    attended = attended.astype(jnp.bfloat16).reshape(-1, chans)
    update = jnp.dot(attended, out_weight, preferred_element_type=jnp.float32).astype(jnp.bfloat16)
    return update.reshape(count, cells, chans)

def reference(coded, tile_scales, expand_weight, expand_bias, depth_kernel, depth_bias, project_weight, project_bias, query_weight, key_weight, value_weight, out_weight):
    scale_full = jnp.repeat(jnp.repeat(tile_scales, TILE, axis=0), TILE, axis=1)
    x_in = (coded.astype(jnp.float32) * scale_full).astype(jnp.bfloat16)
    padded = jnp.pad(x_in, ((1, 1), (1, 1), (0, 0)))
    row_index = jnp.arange(ROWS + 2)
    col_index = jnp.arange(COLS + 2)
    row_valid = (row_index >= 1) & (row_index <= ROWS)
    col_valid = (col_index >= 1) & (col_index <= COLS)

    def band(number):
        start = (number * TILE).astype(jnp.int32)
        piece = lax.dynamic_slice_in_dim(padded, start, TILE + 2, 0)
        rows_ok = lax.dynamic_slice_in_dim(row_valid, start, TILE + 2, 0)
        pre = jnp.dot(piece.reshape(-1, C), expand_weight, preferred_element_type=jnp.float32)
        pre = pre.reshape(TILE + 2, COLS + 2, FF) + expand_bias
        inside = rows_ok[:, None, None] & col_valid[None, :, None]
        expanded = jnp.where(inside, gelu(pre), jnp.float32(0.0)).astype(jnp.bfloat16)
        total = jnp.zeros((TILE, COLS, FF), jnp.float32)
        for shift_y in range(3):
            for shift_x in range(3):
                total = total + depth_kernel[3 * shift_y + shift_x] * expanded[shift_y:shift_y + TILE, shift_x:shift_x + COLS].astype(jnp.float32)
        depth = gelu(total + depth_bias).astype(jnp.bfloat16)
        proj = jnp.dot(depth.reshape(-1, FF), project_weight, preferred_element_type=jnp.float32)
        home = lax.dynamic_slice_in_dim(x_in, start, TILE, 0)
        return (home.astype(jnp.float32) + proj.reshape(TILE, COLS, C) + project_bias).astype(jnp.bfloat16)
    mixed = lax.map(band, jnp.arange(ROWS // TILE, dtype=jnp.int32)).reshape(ROWS, COLS, C)
    tiles = mixed.reshape(GRID, ROWS // GRID, GRID, COLS // GRID, C).transpose(1, 3, 0, 2, 4)
    tiles = tiles.reshape(ROWS // GRID, COLS // GRID, GRID * GRID, C)
    updates = lax.map(lambda grp: attend(grp, query_weight, key_weight, value_weight, out_weight), tiles)
    updates = updates.reshape(ROWS // GRID, COLS // GRID, GRID, GRID, C).transpose(2, 0, 3, 1, 4).reshape(ROWS, COLS, C)
    return (mixed.astype(jnp.float32) + updates.astype(jnp.float32)).astype(jnp.bfloat16)
```

```python
import jax
import jax.numpy as jnp
from jax import lax
from jax.experimental import pallas as pl
from jax.experimental.pallas import tpu as pltpu
from jax.sharding import PartitionSpec as P

HEAD_DIM = 32
HEADS = 8
GRID = 8
TILE = 8
LANES = 16
STEP = 6
SLOTS = STEP + 2
PAD = 112
CHUNK = 4

A = 0.7978845608028654
B = A * 0.044715
U = B ** (1.0 / 3.0)
BF = jnp.bfloat16
F32 = jnp.float32


def scaled_gelu(y):
    t = jnp.tanh(y * (y * y + jnp.asarray(A / U, y.dtype)))
    return y * t + y


def mb_kernel(
    coded_ref,
    scale_ref,
    ext_ref,
    lr_ref,
    edge_ref,
    we_ref,
    be_ref,
    taps_ref,
    bd_ref,
    wp_ref,
    bp_ref,
    out_ref,
    xs_ref,
    lhs_ref,
    e_ref,
    xk_ref,
    dp_ref,
):
    step = pl.program_id(0)
    last = pl.num_programs(0) - 1
    rows = coded_ref.shape[0]
    cols = STEP * LANES
    width = we_ref.shape[1]

    def gather(at, keep):
        for slot in range(SLOTS):
            wide = jnp.concatenate(
                [xs_ref[at, half, pl.ds(7 + slot, LANES, stride=STEP), :] for half in range(2)],
                axis=1,
            )
            place = at * SLOTS * LANES + slot * LANES
            lhs_ref[pl.ds(place, LANES), :] = (wide * U).astype(BF)
            if keep is not None and 1 <= slot <= STEP:
                xk_ref[keep, pl.ds((slot - 1) * LANES, LANES), :] = wide.astype(BF)

    def expand(count, first, mask):
        for part in range(width // 256):
            cut = slice(part * 256, part * 256 + 256)
            pre = jnp.dot(
                lhs_ref[0 : count * SLOTS * LANES, :], we_ref[:, cut], preferred_element_type=F32
            )
            act = scaled_gelu((pre + be_ref[:, cut]).astype(BF))
            act = act.reshape(count, SLOTS, LANES, 256)
            if mask is not None:
                act = act * edge_ref[mask, :, cut]
            e_ref[pl.ds(first, count), 0:1, :, cut] = act[:, 0:1] * edge_ref[0, :, cut]
            e_ref[pl.ds(first, count), 1 : SLOTS - 1, :, cut] = act[:, 1 : SLOTS - 1]
            e_ref[pl.ds(first, count), SLOTS - 1 :, :, cut] = act[:, SLOTS - 1 :] * edge_ref[1, :, cut]

    def outer_row(which, first):
        for half in range(2):
            xs_ref[0, half] = ext_ref[which, :, half * 128 : half * 128 + 128]
        gather(0, None)
        expand(1, first, 2 + which)

    @pl.when(step == 0)
    def _():
        outer_row(0, 0)

    @pl.when(step == last)
    def _():
        outer_row(1, last * rows + 1)

    def expand_chunk(piece):
        base = piece * CHUNK
        scales = scale_ref[0][:, None, :]
        for row in range(CHUNK):
            wide = coded_ref[base + row].astype(F32).reshape(cols // TILE, TILE, 256) * scales
            wide = wide.reshape(cols, 256)
            for half in range(2):
                lanes = slice(half * 128, half * 128 + 128)
                xs_ref[row, half, 8 : 8 + cols, :] = wide[:, lanes]
                xs_ref[row, half, 7:8, :] = lr_ref[base + row, 0:1, lanes]
                xs_ref[row, half, 8 + cols : 9 + cols, :] = lr_ref[base + row, 1:2, lanes]
            gather(row, step * rows + base + row)
        expand(CHUNK, step * rows + base + 1, None)

    def depth_chunk(piece):
        base = piece * CHUNK
        first = (step - 1) * rows + base
        for part in range(width // 128):
            cut = slice(part * 128, part * 128 + 128)
            for row in range(CHUNK):
                total = None
                for dy in range(3):
                    line = e_ref[first + row + dy, :, :, cut]
                    for dx in range(3):
                        term = line[dx : dx + STEP] * taps_ref[3 * dy + dx, :, cut]
                        total = term if total is None else total + term
                act = scaled_gelu(total + bd_ref[:, cut])
                dp_ref[row * cols : (row + 1) * cols, cut] = act.reshape(cols, 128)
        proj = jnp.dot(dp_ref[...], wp_ref[...], preferred_element_type=F32)
        home = xk_ref[pl.ds(first, CHUNK)].astype(F32).reshape(CHUNK * cols, 256)
        mixed = home + (proj * (0.5 / U) + bp_ref[...])
        out_ref[pl.ds(base, CHUNK)] = mixed.astype(BF).reshape(CHUNK, cols, 256)

    for piece in range(rows // CHUNK):

        @pl.when(step < last)
        def _(piece=piece):
            expand_chunk(piece)

        @pl.when(step > 0)
        def _(piece=piece):
            depth_chunk(piece)


def mb_call(coded, scales, ext, lr, edge, we, be, taps, bd, wp, bp):
    rows, cols, chans = coded.shape
    width = we.shape[1]
    block = TILE
    steps = rows // block

    def whole(array):
        return pl.BlockSpec(array.shape, lambda i, n=array.ndim: (0,) * n)

    def ahead(i):
        return jnp.minimum(i, steps - 1)

    return pl.pallas_call(
        mb_kernel,
        grid=(steps + 1,),
        out_shape=jax.ShapeDtypeStruct((rows, cols, chans), BF),
        in_specs=[
            pl.BlockSpec((block, cols, chans), lambda i: (ahead(i), 0, 0)),
            pl.BlockSpec((1, cols // TILE, chans), lambda i: (ahead(i), 0, 0)),
            whole(ext),
            pl.BlockSpec((block, 2, chans), lambda i: (ahead(i), 0, 0)),
            whole(edge),
            whole(we),
            whole(be),
            whole(taps),
            whole(bd),
            whole(wp),
            whole(bp),
        ],
        out_specs=pl.BlockSpec((block, cols, chans), lambda i: (jnp.maximum(i - 1, 0), 0, 0)),
        scratch_shapes=[
            pltpu.VMEM((CHUNK, 2, PAD, 128), F32),
            pltpu.VMEM((CHUNK * SLOTS * LANES, chans), BF),
            pltpu.VMEM((rows + 2, SLOTS, LANES, width), BF),
            pltpu.VMEM((rows, cols, chans), BF),
            pltpu.VMEM((CHUNK * cols, width), BF),
        ],
        compiler_params=pltpu.CompilerParams(vmem_limit_bytes=48 * 1024 * 1024),
        cost_estimate=pl.CostEstimate(
            flops=4 * rows * cols * chans * width,
            bytes_accessed=4 * rows * cols * chans,
            transcendentals=2 * rows * cols * width,
        ),
    )(coded, scales, ext, lr, edge, we, be, taps, bd, wp, bp)


def attend_kernel(m_ref, wqkv_ref, wo_ref, mask_ref, out_ref, n_ref, q_ref, k_ref, v_ref, a_ref, u_ref):
    cells, count, chans = m_ref.shape
    total = cells * count
    m = m_ref[...].astype(F32).reshape(total, chans)
    center = jnp.mean(m, axis=-1, keepdims=True)
    apart = m - center
    spread = jnp.mean(apart * apart, axis=-1, keepdims=True)
    normed = apart * lax.rsqrt(spread + 1e-05)
    for half in range(2):
        n_ref[half] = normed[:, half * 128 : half * 128 + 128]
    qscale = float(HEAD_DIM**-0.5 * 1.4426950408889634)
    some = 4
    for at in range(0, count, some):
        tall = jnp.concatenate(
            [
                jnp.concatenate(
                    [n_ref[half, pl.ds(g, cells, stride=count), :] for half in range(2)], axis=1
                )
                for g in range(at, at + some)
            ],
            axis=0,
        ).astype(BF)
        qkv = jnp.dot(tall, wqkv_ref[...], preferred_element_type=F32)
        here = slice(at * cells, (at + some) * cells)
        q_ref[here, :] = (qkv[:, :chans] * qscale).astype(BF)
        k_ref[here, :] = qkv[:, chans : 2 * chans]
        v_ref[here, :] = qkv[:, 2 * chans :]

    def spread_heads(ref, base):
        tall = jnp.concatenate(
            [jnp.broadcast_to(ref[pl.ds(base + key, 1), :], (HEADS, chans)) for key in range(cells)],
            axis=0,
        ).astype(BF)
        tall = tall.reshape(cells // 2, 2 * HEADS, chans) * mask_ref[...]
        return tall.reshape(cells * HEADS, chans)

    def fold(array, op):
        out = array[:, 0:128]
        for part in range(1, array.shape[1] // 128):
            out = op(out, array[:, part * 128 : part * 128 + 128])
        for shift in (64, 32, 16, 8):
            out = op(out, pltpu.roll(out, shift, 1))
        return out

    def one_group(g):
        base = pl.multiple_of(g * cells, cells)
        keys = spread_heads(k_ref, base)
        scores = lax.dot_general(
            q_ref[pl.ds(base, cells), :],
            keys,
            (((1,), (1,)), ((), ())),
            preferred_element_type=F32,
        )
        wide = scores.shape[1] // 128
        top = fold(scores, jnp.maximum)
        raw = jnp.exp2(scores - jnp.concatenate([top] * wide, axis=1))
        under = 1.0 / fold(raw, jnp.add)
        weights = (raw * jnp.concatenate([under] * wide, axis=1)).astype(BF)
        values = spread_heads(v_ref, base)
        attended = jnp.dot(weights, values, preferred_element_type=F32)
        a_ref[pl.ds(base, cells), :] = attended.astype(BF)

    together = 4

    @pl.loop(0, count // together)
    def _(turn):
        for one in range(together):
            one_group(turn * together + one)

    for at in range(0, count, some):
        here = slice(at * cells, (at + some) * cells)
        update = jnp.dot(a_ref[here, :], wo_ref[...], preferred_element_type=F32)
        for g in range(some):
            for half in range(2):
                u_ref[half, pl.ds(at + g, cells, stride=count), :] = update[
                    g * cells : (g + 1) * cells, half * 128 : half * 128 + 128
                ]
    for half in range(2):
        out_ref[:, :, half * 128 : half * 128 + 128] = (
            u_ref[half].astype(BF).reshape(cells, count, 128)
        )


def attend_call(moved, wqkv, wo, mask):
    cells, groups, chans = moved.shape
    count = 16
    total = cells * count
    return pl.pallas_call(
        attend_kernel,
        grid=(groups // count,),
        out_shape=jax.ShapeDtypeStruct(moved.shape, BF),
        in_specs=[
            pl.BlockSpec((cells, count, chans), lambda i: (0, i, 0)),
            pl.BlockSpec(wqkv.shape, lambda i: (0, 0)),
            pl.BlockSpec(wo.shape, lambda i: (0, 0)),
            pl.BlockSpec(mask.shape, lambda i: (0, 0)),
        ],
        out_specs=pl.BlockSpec((cells, count, chans), lambda i: (0, i, 0)),
        scratch_shapes=[
            pltpu.VMEM((2, total, 128), F32),
            pltpu.VMEM((total, chans), BF),
            pltpu.VMEM((total, chans), F32),
            pltpu.VMEM((total, chans), F32),
            pltpu.VMEM((total, chans), BF),
            pltpu.VMEM((2, total, 128), F32),
        ],
        compiler_params=pltpu.CompilerParams(vmem_limit_bytes=48 * 1024 * 1024),
        cost_estimate=pl.CostEstimate(
            flops=2 * cells * groups * chans * (4 * chans + 4 * cells),
            bytes_accessed=4 * cells * groups * chans,
            transcendentals=cells * groups * cells * HEADS,
        ),
    )(moved, wqkv, wo, mask)


def finish_kernel(mixed_ref, home_ref, out_ref, line_ref):
    for row in range(mixed_ref.shape[0]):
        for half in range(2):
            lanes = slice(half * 128, half * 128 + 128)
            for slot in range(STEP):
                here = slice(slot * LANES, (slot + 1) * LANES)
                line_ref[half, pl.ds(slot, LANES, stride=STEP), :] = mixed_ref[
                    row, here, lanes
                ].astype(F32) + home_ref[row, here, lanes].astype(F32)
            out_ref[row, :, lanes] = line_ref[half].astype(BF)


def finish_call(mixed, home):
    rows, cols, chans = mixed.shape
    block = 8
    spec = pl.BlockSpec((block, cols, chans), lambda i: (i, 0, 0))
    return pl.pallas_call(
        finish_kernel,
        grid=(rows // block,),
        out_shape=jax.ShapeDtypeStruct(mixed.shape, BF),
        in_specs=[spec, spec],
        out_specs=spec,
        scratch_shapes=[pltpu.VMEM((2, cols, 128), F32)],
        cost_estimate=pl.CostEstimate(
            flops=rows * cols * chans, bytes_accessed=6 * rows * cols * chans, transcendentals=0
        ),
    )(mixed, home)


def dequant(coded, scales):
    return (coded.astype(F32) * scales).astype(BF)


def halo(coded, tile_scales):
    rows, cols, _ = coded.shape
    wide = [jnp.repeat(tile_scales[at], TILE, axis=0) for at in (0, -1)]
    tall = [jnp.repeat(tile_scales[:, at], TILE, axis=0) for at in (0, -1)]
    edge_top, edge_bottom = dequant(coded[0], wide[0]), dequant(coded[-1], wide[1])
    edge_left, edge_right = dequant(coded[:, 0], tall[0]), dequant(coded[:, -1], tall[1])

    def swap(axis, low, high):
        peers = lax.axis_size(axis)
        up = [(i, i + 1) for i in range(peers - 1)]
        down = [(i + 1, i) for i in range(peers - 1)]
        return lax.ppermute(high, axis, up), lax.ppermute(low, axis, down)

    above, below = swap("gy", edge_top, edge_bottom)
    low = jnp.concatenate([above[:1], edge_left, below[:1]], axis=0)
    high = jnp.concatenate([above[-1:], edge_right, below[-1:]], axis=0)
    left, right = swap("gx", low, high)
    return above, below, left, right


def per_device(
    coded,
    tile_scales,
    expand_weight,
    expand_bias,
    depth_kernel,
    depth_bias,
    project_weight,
    project_bias,
    query_weight,
    key_weight,
    value_weight,
    out_weight,
):
    rows, cols, chans = coded.shape
    width = expand_weight.shape[1]
    above, below, left, right = halo(coded, tile_scales)

    def outer(line, at):
        return jnp.pad(
            jnp.concatenate([left[at : at + 1], line, right[at : at + 1]], axis=0),
            ((7, PAD - 9 - cols), (0, 0)),
        ).astype(F32)

    ext = jnp.stack([outer(above, 0), outer(below, rows + 1)])
    lr = jnp.stack([left[1:-1], right[1:-1]], axis=1).astype(F32)
    gy, gx = lax.axis_index("gy"), lax.axis_index("gx")
    lane = jnp.arange(LANES)
    inside = jnp.stack(
        [
            (lane > 0) | (gx > 0),
            (lane < LANES - 1) | (gx < lax.axis_size("gx") - 1),
            jnp.broadcast_to(gy > 0, (LANES,)),
            jnp.broadcast_to(gy < lax.axis_size("gy") - 1, (LANES,)),
        ]
    )
    edge = jnp.broadcast_to(inside[:, :, None], (4, LANES, width)).astype(BF)
    taps = jnp.broadcast_to((depth_kernel * 0.5).astype(BF)[:, None, :], (9, LANES, width))
    bd = jnp.broadcast_to((depth_bias * U).astype(BF)[None, :], (LANES, width))
    mixed = mb_call(
        coded,
        tile_scales,
        ext,
        lr,
        edge,
        expand_weight,
        (expand_bias * U)[None, :],
        taps,
        bd,
        project_weight,
        project_bias[None, :],
    )
    wide = lax.axis_size("gx")
    peers = lax.axis_size("gy") * wide
    parity = [[d for d in range(peers) if d % 2 == core] for core in range(2)]

    def exchange(array):
        return lax.all_to_all(
            array, ("gy", "gx"), 0, 0, tiled=True, axis_index_groups=parity
        )

    wqkv = jnp.concatenate([query_weight, key_weight, value_weight], axis=1)
    head = jnp.arange(chans)[None, :] // HEAD_DIM
    mask = (head == (jnp.arange(2 * HEADS) % HEADS)[:, None]).astype(BF)
    update = attend_call(exchange(mixed), wqkv, out_weight, mask)
    return finish_call(mixed, exchange(update))


def solution(mesh):
    return jax.shard_map(
        per_device,
        mesh=mesh,
        in_specs=(
            P("gy", "gx", None),
            P("gy", "gx", None),
            P(),
            P(),
            P(),
            P(),
            P(),
            P(),
            P(),
            P(),
            P(),
            P(),
        ),
        out_specs=P("gy", "gx", None),
        check_vma=False,
    )
```

```python
import functools

import jax
import jax.numpy as jnp
from jax import lax
from jax.experimental import pallas as pl
from jax.experimental.pallas import tpu as pltpu
from jax.sharding import PartitionSpec as P

HEAD_DIM = 32
HEADS = 8
TILE = 8
LANES = 8
STEP = 12
SLOTS = STEP + 2
PAD = 112
BLOCK = 8
CHUNK = 4
RING = 24
PARTS = 2

A = 0.7978845608028654
B = A * 0.044715
U = B ** (1.0 / 3.0)
VMEM = 63 * 1024 * 1024
BF = jnp.bfloat16
F32 = jnp.float32


def scaled_gelu(y):
    t = jnp.tanh(y * (y * y + A / U))
    return y * t + y

def mb_kernel(
    top_out,
    bottom_out,
    first_row,
    coded_ref,
    scale_ref,
    top_ref,
    bottom_ref,
    topscale_ref,
    bottomscale_ref,
    left_ref,
    right_ref,
    we_ref,
    be_ref,
    dk_ref,
    bd_ref,
    wp_ref,
    bp_ref,
    out_ref,
    xs_ref,
    lhs_ref,
    e_ref,
    xk_ref,
    dp_ref,
    taps_ref,
    beu_ref,
    bdu_ref,
    lr_ref,
    line_ref,
):
    step = pl.program_id(0)
    last = pl.num_programs(0) - 1
    rows, cols, chans = coded_ref.shape
    width = we_ref.shape[1]
    gy, gx = lax.axis_index("gy"), lax.axis_index("gx")

    @pl.when(step == 0)
    def _():
        for n in range(9):
            taps_ref[n] = jnp.broadcast_to(dk_ref[n : n + 1, :] * 0.5, (8, width))
        beu_ref[...] = jnp.broadcast_to(be_ref[...] * U, (8, width))
        bdu_ref[...] = jnp.broadcast_to(bd_ref[...] * U, (8, width))
        for half in range(2):
            lanes = slice(half * 128, half * 128 + 128)
            lr_ref[0, half] = left_ref[:, lanes].astype(F32)
            lr_ref[1, half] = right_ref[:, lanes].astype(F32)

    lane = lax.broadcasted_iota(jnp.int32, (8, 256), 0)
    one, nil = jnp.float32(1), jnp.float32(0)
    tall_devs, wide_devs = lax.axis_size("gy"), lax.axis_size("gx")
    edge_left = jnp.where((lane > 0) | (gx > 0), one, nil)
    edge_right = jnp.where((lane < 7) | (gx < wide_devs - 1), one, nil)

    def ring(row):
        return lax.rem(row + 1, RING)

    def fill(at, wide, row):
        for half in range(2):
            lanes = slice(half * 128, half * 128 + 128)
            xs_ref[at, half, 8 : 8 + cols, :] = wide[:, lanes]
            xs_ref[at, half, 7:8, :] = lr_ref[0, half, pl.ds(first_row + row + 1, 1), :]
            xs_ref[at, half, 8 + cols : 9 + cols, :] = lr_ref[1, half, pl.ds(first_row + row + 1, 1), :]

    def gather(at, keep):
        slots = []
        for slot in range(SLOTS):
            slots.append(jnp.concatenate(
                [xs_ref[at, half, pl.ds(7 + slot, LANES, stride=STEP), :] for half in range(2)], axis=1))
        tall = jnp.concatenate(slots, axis=0)
        lhs_ref[pl.ds(at * SLOTS * LANES, SLOTS * LANES), :] = (tall * U).astype(BF)
        if keep is not None:
            xk_ref[lax.rem(keep, 2 * BLOCK)] = tall[LANES : LANES + cols].astype(BF)

    def expand(count, row, scale):
        for part in range(width // 256):
            cut = slice(part * 256, part * 256 + 256)
            pre = jnp.dot(lhs_ref[0 : count * SLOTS * LANES, :], we_ref[:, cut], preferred_element_type=F32)
            act = scaled_gelu(pre.reshape(count * SLOTS, LANES, 256) + beu_ref[:, cut])
            act = act.reshape(count, SLOTS, LANES, 256)
            if scale is not None:
                act = act * scale
            for at in range(count):
                pos = ring(row + at)
                e_ref[pos, 0, :, cut] = act[at, 0] * edge_left
                e_ref[pos, 1 : SLOTS - 1, :, cut] = act[at, 1 : SLOTS - 1]
                e_ref[pos, SLOTS - 1, :, cut] = act[at, SLOTS - 1] * edge_right

    def dequant(coded, scales):
        wide = coded.astype(F32).reshape(cols // TILE, TILE, chans) * scales[:, None, :]
        return wide.reshape(cols, chans)

    def outer_row(ref, scale, outside, row, inside):
        if outside:
            fill(0, ref[0].astype(F32), row)
        else:
            fill(0, dequant(ref[0], scale[0]), row)
        gather(0, None)
        expand(1, row, jnp.where(inside, one, nil) if outside else None)

    @pl.when(step == 0)
    def _():
        outer_row(top_ref, topscale_ref, top_out, -1, gy > 0)

    @pl.when(step == last)
    def _():
        outer_row(bottom_ref, bottomscale_ref, bottom_out, last * rows, gy < tall_devs - 1)

    def expand_chunk(piece):
        base = piece * CHUNK
        for at in range(CHUNK):
            row = step * rows + base + at
            fill(at, dequant(coded_ref[base + at], scale_ref[0]), row)
            gather(at, row)
        expand(CHUNK, step * rows + base, None)

    def depth_chunk(piece):
        base = piece * CHUNK
        first = (step - 1) * rows + base
        for part in range(width // 128):
            cut = slice(part * 128, part * 128 + 128)
            taps = [taps_ref[n, :, cut] for n in range(9)]
            for at in range(CHUNK):
                total = bdu_ref[:, cut]
                for dy in range(3):
                    line = e_ref[ring(first + at + dy - 1), :, :, cut]
                    for dx in range(3):
                        total = total + line[dx : dx + STEP] * taps[3 * dy + dx]
                act = scaled_gelu(total)
                dp_ref[at * cols : (at + 1) * cols, cut] = act.reshape(cols, 128).astype(BF)
        proj = jnp.dot(dp_ref[...], wp_ref[...], preferred_element_type=F32)
        proj = proj * (0.5 / U) + bp_ref[...]
        for at in range(CHUNK):
            home = xk_ref[lax.rem(first + at, 2 * BLOCK)].astype(F32)
            mixed = home + proj[at * cols : (at + 1) * cols]
            for half in range(2):
                lanes = slice(half * 128, half * 128 + 128)
                for slot in range(STEP):
                    line_ref[at, half, pl.ds(slot, LANES, stride=STEP), :] = mixed[slot * LANES : slot * LANES + LANES, lanes]
                out_ref[base + at, :, lanes] = line_ref[at, half].astype(BF)

    for piece in range(BLOCK // CHUNK):

        @pl.when(step < last)
        def _(piece=piece):
            expand_chunk(piece)

        @pl.when(step > 0)
        def _(piece=piece):
            depth_chunk(piece)

def mb_call(coded, scales, above, below, left, right, we, be, dk, bd, wp, bp, first, count):
    rows, cols, chans = coded.shape
    width = we.shape[1]
    steps = count // BLOCK
    skip = first // BLOCK
    top_out, bottom_out = first == 0, first + count == rows
    def whole(array):
        return pl.BlockSpec(array.shape, lambda i, n=array.ndim: (0,) * n)
    def ahead(i):
        return skip + jnp.minimum(i, steps - 1)
    line = (1, cols, chans)
    def outer(outside, halo, row):
        if outside:
            return halo.reshape(line), pl.BlockSpec(line, lambda i: (0, 0, 0)), 0
        return coded, pl.BlockSpec(line, lambda i: (row, 0, 0)), row // TILE
    top, top_spec, top_tile = outer(top_out, above, first - 1)
    bottom, bottom_spec, bottom_tile = outer(bottom_out, below, first + count)
    return pl.pallas_call(
        functools.partial(mb_kernel, top_out, bottom_out, first),
        grid=(steps + 1,),
        out_shape=jax.ShapeDtypeStruct((count, cols, chans), BF),
        in_specs=[
            pl.BlockSpec((BLOCK, cols, chans), lambda i: (ahead(i), 0, 0)),
            pl.BlockSpec((1, cols // TILE, chans), lambda i: (ahead(i), 0, 0)),
            top_spec, bottom_spec,
            pl.BlockSpec((1, cols // TILE, chans), lambda i: (top_tile, 0, 0)),
            pl.BlockSpec((1, cols // TILE, chans), lambda i: (bottom_tile, 0, 0)),
            whole(left), whole(right), whole(we), whole(be), whole(dk), whole(bd), whole(wp), whole(bp),
        ],
        out_specs=pl.BlockSpec((BLOCK, cols, chans), lambda i: (jnp.maximum(i - 1, 0), 0, 0)),
        scratch_shapes=[
            pltpu.VMEM((CHUNK, 2, PAD, 128), F32),
            pltpu.VMEM((CHUNK * SLOTS * LANES, chans), BF),
            pltpu.VMEM((RING, SLOTS, LANES, width), F32),
            pltpu.VMEM((2 * BLOCK, cols, chans), BF),
            pltpu.VMEM((CHUNK * cols, width), BF),
            pltpu.VMEM((9, 8, width), F32),
            pltpu.VMEM((8, width), F32),
            pltpu.VMEM((8, width), F32),
            pltpu.VMEM((2, 2, left.shape[0], 128), F32),
            pltpu.VMEM((CHUNK, 2, cols, 128), F32),
        ],
        compiler_params=pltpu.CompilerParams(vmem_limit_bytes=VMEM),
        cost_estimate=pl.CostEstimate(
            flops=4 * count * cols * chans * width,
            bytes_accessed=4 * count * cols * chans,
            transcendentals=2 * count * cols * width,
        ),
    )(coded, scales, top, bottom, scales, scales, left, right, we, be, dk, bd, wp, bp)


def attend_kernel(
    m_ref,
    wq_ref,
    wk_ref,
    wv_ref,
    wo_ref,
    kmask_ref,
    vmask_ref,
    ones_ref,
    out_ref,
    n_ref,
    q_ref,
    k_ref,
    v_ref,
    p_ref,
    a_ref,
    u_ref,
):
    cells, count, chans = m_ref.shape
    total = cells * count
    pairs = HEADS // 2
    m = m_ref[...].astype(F32).reshape(total, chans)
    center = jnp.mean(m, axis=-1, keepdims=True)
    apart = m - center
    spread = jnp.mean(apart * apart, axis=-1, keepdims=True)
    normed = apart * lax.rsqrt(spread + 1e-05)
    for half in range(2):
        n_ref[half] = normed[:, half * 128 : half * 128 + 128]
    qscale = float(HEAD_DIM**-0.5 * 1.4426950408889634)
    tall = jnp.concatenate(
        [
            jnp.concatenate(
                [n_ref[half, pl.ds(g, cells, stride=count), :] for half in range(2)], axis=1
            )
            for g in range(count)
        ],
        axis=0,
    ).astype(BF)
    q_ref[...] = (jnp.dot(tall, wq_ref[...], preferred_element_type=F32) * qscale).astype(BF)
    k_ref[...] = jnp.dot(tall, wk_ref[...], preferred_element_type=F32).astype(BF)
    v_ref[...] = jnp.dot(tall, wv_ref[...], preferred_element_type=F32).astype(BF)

    blank = jnp.zeros((64, 128), BF)
    tall = []
    for g in range(count):
        here = slice(g * cells, (g + 1) * cells)
        k = k_ref[here, :]
        kt = jnp.concatenate([k, k], axis=0).T * kmask_ref[...]
        q = q_ref[here, :]
        parts = []
        for side in range(2):
            lanes = slice(side * 128, side * 128 + 128)
            upper, lower = kt[side * 128 : side * 128 + 64], kt[side * 128 + 64 : side * 128 + 128]
            keys = jnp.concatenate(
                [
                    jnp.concatenate([upper, blank], axis=0),
                    jnp.concatenate([blank, lower], axis=0),
                ],
                axis=1,
            )
            parts.append(jnp.dot(q[:, lanes], keys, preferred_element_type=F32))
        tall.append(jnp.concatenate(parts, axis=1))
    scores = jnp.concatenate(tall, axis=0)
    first = lax.broadcasted_iota(jnp.int32, (1, 128), 1) < 64
    low = jnp.float32(-jnp.inf)
    for pair in range(pairs):
        lanes = slice(pair * 128, pair * 128 + 128)
        two = scores[:, lanes]
        top = jnp.where(
            first,
            jnp.max(jnp.where(first, two, low), axis=-1, keepdims=True),
            jnp.max(jnp.where(first, low, two), axis=-1, keepdims=True),
        )
        p_ref[:, lanes] = jnp.exp2(two - top).astype(BF)
    for g in range(count):
        here = slice(g * cells, (g + 1) * cells)
        for side in range(2):
            lanes = slice(side * 128, side * 128 + 128)
            v = v_ref[here, lanes]
            values = jnp.concatenate(
                [v * vmask_ref[h, :, lanes] for h in range(4 * side, 4 * side + 4)], axis=0
            )
            a_ref[here, lanes] = jnp.dot(
                p_ref[here, side * 256 : side * 256 + 256], values, preferred_element_type=F32
            )
    under = jnp.dot(p_ref[...], ones_ref[...], preferred_element_type=F32)
    attended = (a_ref[...] / under).astype(BF)
    update = jnp.dot(attended, wo_ref[...], preferred_element_type=F32)
    for g in range(count):
        for half in range(2):
            u_ref[half, pl.ds(g, cells, stride=count), :] = update[
                g * cells : (g + 1) * cells, half * 128 : half * 128 + 128
            ]
    for half in range(2):
        out_ref[:, :, half * 128 : half * 128 + 128] = (
            u_ref[half].astype(BF).reshape(cells, count, 128)
        )


def attend_call(moved, wq, wk, wv, wo):
    cells, groups, chans = moved.shape
    count = 16
    total = cells * count
    chan, lane = jnp.arange(chans), jnp.arange(128)
    kmask = ((chan[:, None] // HEAD_DIM) % 2 == lane[None, :] // 64).astype(BF)
    head = jnp.arange(HEADS)
    vmask = jnp.broadcast_to(
        chan[None, None, :] // HEAD_DIM == head[:, None, None], (HEADS, cells, chans)
    ).astype(BF)
    ones = (chan[None, :] // HEAD_DIM == jnp.arange(HEADS * cells)[:, None] // cells).astype(BF)

    def whole(array):
        return pl.BlockSpec(array.shape, lambda i, n=array.ndim: (0,) * n)

    return pl.pallas_call(
        attend_kernel,
        grid=(groups // count,),
        out_shape=jax.ShapeDtypeStruct(moved.shape, BF),
        in_specs=[
            pl.BlockSpec((cells, count, chans), lambda i: (0, i, 0)),
            *[whole(a) for a in (wq, wk, wv, wo, kmask, vmask, ones)],
        ],
        out_specs=pl.BlockSpec((cells, count, chans), lambda i: (0, i, 0)),
        scratch_shapes=[
            pltpu.VMEM((2, total, 128), F32),
            pltpu.VMEM((total, chans), BF),
            pltpu.VMEM((total, chans), BF),
            pltpu.VMEM((total, chans), BF),
            pltpu.VMEM((total, HEADS * cells), BF),
            pltpu.VMEM((total, chans), F32),
            pltpu.VMEM((2, total, 128), F32),
        ],
        compiler_params=pltpu.CompilerParams(vmem_limit_bytes=VMEM),
        cost_estimate=pl.CostEstimate(
            flops=2 * cells * groups * chans * (4 * chans + 4 * cells),
            bytes_accessed=4 * cells * groups * chans,
            transcendentals=cells * groups * cells * HEADS,
        ),
    )(moved, wq, wk, wv, wo, kmask, vmask, ones)


def dequant(coded, scales):
    return (coded.astype(F32) * scales).astype(BF)


def halo(coded, tile_scales):
    wide = [jnp.repeat(tile_scales[at], TILE, axis=0) for at in (0, -1)]
    tall = [jnp.repeat(tile_scales[:, at], TILE, axis=0) for at in (0, -1)]
    edge_top, edge_bottom = dequant(coded[0], wide[0]), dequant(coded[-1], wide[1])
    edge_left, edge_right = dequant(coded[:, 0], tall[0]), dequant(coded[:, -1], tall[1])

    def swap(axis, low, high):
        peers = lax.axis_size(axis)
        up = [(i, i + 1) for i in range(peers - 1)]
        down = [(i + 1, i) for i in range(peers - 1)]
        return lax.ppermute(high, axis, up), lax.ppermute(low, axis, down)

    above, below = swap("gy", edge_top, edge_bottom)
    low = jnp.concatenate([above[:1], edge_left, below[:1]], axis=0)
    high = jnp.concatenate([above[-1:], edge_right, below[-1:]], axis=0)
    left, right = swap("gx", low, high)
    return above, below, left, right


def per_device(
    coded,
    tile_scales,
    expand_weight,
    expand_bias,
    depth_kernel,
    depth_bias,
    project_weight,
    project_bias,
    query_weight,
    key_weight,
    value_weight,
    out_weight,
):
    rows, cols, chans = coded.shape
    around = halo(coded, tile_scales)
    wide = lax.axis_size("gx")
    peers = lax.axis_size("gy") * wide
    parity = [[d for d in range(peers) if d % 2 == core] for core in range(2)]

    def exchange(array):
        return lax.all_to_all(array, ("gy", "gx"), 0, 0, tiled=True, axis_index_groups=parity)

    count = rows // PARTS
    share = (peers // 2, cols * count * 2 // peers, chans)
    out = []
    for part in range(PARTS):
        mixed = mb_call(
            coded,
            tile_scales,
            *around,
            expand_weight,
            expand_bias[None, :],
            depth_kernel,
            depth_bias[None, :],
            project_weight,
            project_bias[None, :],
            first=part * count,
            count=count,
        )
        moved = exchange(mixed.reshape(share))
        update = attend_call(moved, query_weight, key_weight, value_weight, out_weight)
        home = exchange(update).reshape(mixed.shape)
        out.append((mixed.astype(F32) + home.astype(F32)).astype(BF))
    return out[0] if PARTS == 1 else jnp.concatenate(out, axis=0)


def solution(mesh):
    return jax.shard_map(
        per_device,
        mesh=mesh,
        in_specs=(P("gy", "gx", None), P("gy", "gx", None), *[P()] * 10),
        out_specs=P("gy", "gx", None),
        check_vma=False,
    )
```

```python
import functools

import jax
import jax.numpy as jnp
import numpy as np
from jax import lax
from jax.experimental import pallas as pl
from jax.experimental.pallas import tpu as pltpu
from jax.sharding import PartitionSpec as P

HEAD_DIM = 32
HEADS = 8
TILE = 8
LANES = 8
STEP = 12
SLOTS = STEP + 2
PAD = 112
BLOCK = 4
RING = 3 * BLOCK
VMEM = 63 * 1024 * 1024

A = 0.7978845608028654
B = A * 0.044715
U = B ** (1.0 / 3.0)
BF = jnp.bfloat16
F32 = jnp.float32


def scaled_gelu(y):
    t = jnp.tanh(y * (y * y + A / U))
    return y * t + y


def mb_kernel(plan, coded_ref, scale_ref, left_ref, right_ref, *refs):
    segments, first, stride, outside = plan
    refs = list(refs)
    outer = [[refs.pop(0) for _ in range(2)] for _ in outside]
    we_ref, be_ref, dk_ref, bd_ref, wp_ref, bp_ref, out_ref = refs[:7]
    xs_ref, lhs_ref, e_ref, xk_ref, dp_ref, taps_ref, beu_ref, bdu_ref, lr_ref, sc_ref, line_ref = refs[7:]
    step = pl.program_id(0)
    length = pl.num_programs(0) // segments
    segment, k = step // length, lax.rem(step, length)
    last = length - 1
    start = first + segment * stride
    _, cols, chans = coded_ref.shape
    width = we_ref.shape[1]
    gy, gx = lax.axis_index("gy"), lax.axis_index("gx")
    tall_devs, wide_devs = lax.axis_size("gy"), lax.axis_size("gx")
    halves = [slice(0, 128), slice(128, 256)]

    @pl.when(step == 0)
    def _():
        for n in range(9):
            taps_ref[n] = jnp.broadcast_to(dk_ref[n : n + 1, :] * 0.5, (8, width))
        beu_ref[...] = jnp.broadcast_to(be_ref[...] * U, (8, width))
        bdu_ref[...] = jnp.broadcast_to(bd_ref[...] * U, (8, width))
        for half, lanes in enumerate(halves):
            for side, ref in enumerate((left_ref, right_ref)):
                lr_ref[side, half] = ref[:, lanes].astype(F32)
            for col in range(cols // TILE):
                sc_ref[half, pl.ds(col, 8, stride=16), :] = scale_ref[col, :, lanes]

    lane = lax.broadcasted_iota(jnp.int32, (8, 256), 0)
    one, nil = jnp.float32(1), jnp.float32(0)
    edge_left = jnp.where((lane > 0) | (gx > 0), one, nil)
    edge_right = jnp.where((lane < 7) | (gx < wide_devs - 1), one, nil)

    def ring(row):
        return lax.rem(row + 1, RING)

    def fill(at, row, coded, beyond):
        for half, lanes in enumerate(halves):
            x = coded[:, lanes].astype(F32)
            if beyond:
                xs_ref[at, half, 7 : 9 + cols, :] = x
                continue
            tile = pl.multiple_of(row // TILE * 16, 16)
            scales = sc_ref[half, pl.ds(tile, cols // TILE), :]
            x = x.reshape(cols // TILE, TILE, 128) * scales[:, None, :]
            xs_ref[at, half, 8 : 8 + cols, :] = x.reshape(cols, 128)
            xs_ref[at, half, 7:8, :] = lr_ref[0, half, pl.ds(row, 1), :]
            xs_ref[at, half, 8 + cols : 9 + cols, :] = lr_ref[1, half, pl.ds(row, 1), :]

    def gather(at, keep):
        slots = [
            jnp.concatenate(
                [xs_ref[at, half, pl.ds(7 + slot, LANES, stride=STEP), :] for half in range(2)],
                axis=1,
            )
            for slot in range(SLOTS)
        ]
        tall = jnp.concatenate(slots, axis=0)
        lhs_ref[pl.ds(at * SLOTS * LANES, SLOTS * LANES), :] = (tall * U).astype(BF)
        if keep is not None:
            xk_ref[lax.rem(keep, 2 * BLOCK)] = tall[LANES : LANES + cols].astype(BF)

    def expand(count, row, scale):
        for part in range(width // 256):
            cut = slice(part * 256, part * 256 + 256)
            pre = jnp.dot(
                lhs_ref[0 : count * SLOTS * LANES, :], we_ref[:, cut], preferred_element_type=F32
            )
            act = scaled_gelu(pre.reshape(count * SLOTS, LANES, 256) + beu_ref[:, cut])
            act = act.reshape(count, SLOTS, LANES, 256)
            if scale is not None:
                act = act * scale
            for at in range(count):
                pos = ring(row + at)
                e_ref[pos, 0, :, cut] = act[at, 0] * edge_left
                e_ref[pos, 1 : SLOTS - 1, :, cut] = act[at, 1 : SLOTS - 1]
                e_ref[pos, SLOTS - 1, :, cut] = act[at, SLOTS - 1] * edge_right

    def outer_row(ref, beyond, row, inside):
        fill(0, row, ref[0], beyond)
        gather(0, None)
        expand(1, row, jnp.where(inside, one, nil) if beyond else None)

    def expand_block():
        for at in range(BLOCK):
            row = start + k * BLOCK + at
            fill(at, row, coded_ref[at], False)
            gather(at, row)
        expand(BLOCK, start + k * BLOCK, None)

    def depth_block():
        above = start + (k - 1) * BLOCK
        for part in range(width // 128):
            cut = slice(part * 128, part * 128 + 128)
            taps = [taps_ref[n, :, cut] for n in range(9)]
            for at in range(BLOCK):
                total = bdu_ref[:, cut]
                for dy in range(3):
                    line = e_ref[ring(above + at + dy - 1), :, :, cut]
                    for dx in range(3):
                        total = total + line[dx : dx + STEP] * taps[3 * dy + dx]
                act = scaled_gelu(total)
                dp_ref[at * cols : (at + 1) * cols, cut] = act.reshape(cols, 128).astype(BF)
        proj = jnp.dot(dp_ref[...], wp_ref[...], preferred_element_type=F32)
        proj = proj * (0.5 / U) + bp_ref[...]
        for at in range(BLOCK):
            home = xk_ref[lax.rem(above + at, 2 * BLOCK)].astype(F32)
            mixed = home + proj[at * cols : (at + 1) * cols]
            for half, lanes in enumerate(halves):
                for slot in range(STEP):
                    line_ref[at, half, pl.ds(slot, LANES, stride=STEP), :] = mixed[
                        slot * LANES : slot * LANES + LANES, lanes
                    ]
                out_ref[at, :, lanes] = line_ref[at, half].astype(BF)

    for number, (top, bottom) in enumerate(outer):

        @pl.when((segment == number) & (k == 0))
        def _(number=number, top=top):
            outer_row(top, outside[number][0], start - 1, gy > 0)

        @pl.when((segment == number) & (k == last))
        def _(number=number, bottom=bottom):
            outer_row(bottom, outside[number][1], start + last * BLOCK, gy < tall_devs - 1)

    @pl.when(k == 0)
    def _():
        expand_block()

    @pl.when((k > 0) & (k < last))
    def _():
        expand_block()
        depth_block()

    @pl.when(k == last)
    def _():
        depth_block()


def mb_call(coded, scales, rows_beyond, left, right, we, be, dk, bd, wp, bp, firsts, count):
    rows, cols, chans = coded.shape
    width = we.shape[1]
    blocks, segments = count // BLOCK, len(firsts)
    stride = firsts[1] - firsts[0] if segments > 1 else 0
    line = (1, cols, chans)

    def whole(array):
        return pl.BlockSpec(array.shape, lambda i, n=array.ndim: (0,) * n)

    def place(i):
        return i // (blocks + 1), lax.rem(i, blocks + 1)

    def ahead(i):
        segment, k = place(i)
        return (firsts[0] + segment * stride) // BLOCK + jnp.minimum(k, blocks - 1)

    def behind(i):
        segment, k = place(i)
        return segment * blocks + jnp.maximum(k - 1, 0)

    arrays, specs, outside = [], [], []
    for first in firsts:
        outside.append((first == 0, first + count == rows))
        for side, row in enumerate((first - 1, first + count)):
            if outside[-1][side]:
                arrays.append(rows_beyond[side][None])
                specs.append(whole(arrays[-1]))
            else:
                arrays.append(coded)
                specs.append(pl.BlockSpec(line, lambda i, row=row: (row, 0, 0)))
    weights = (we, be, dk, bd, wp, bp)
    cells = count * segments * cols
    return pl.pallas_call(
        functools.partial(mb_kernel, (segments, firsts[0], stride, tuple(outside))),
        grid=(segments * (blocks + 1),),
        out_shape=jax.ShapeDtypeStruct((segments * count, cols, chans), BF),
        in_specs=[
            pl.BlockSpec((BLOCK, cols, chans), lambda i: (ahead(i), 0, 0)),
            whole(scales),
            whole(left),
            whole(right),
            *specs,
            *[whole(a) for a in weights],
        ],
        out_specs=pl.BlockSpec((BLOCK, cols, chans), lambda i: (behind(i), 0, 0)),
        scratch_shapes=[
            pltpu.VMEM((BLOCK, 2, PAD, 128), F32),
            pltpu.VMEM((BLOCK * SLOTS * LANES, chans), BF),
            pltpu.VMEM((RING, SLOTS, LANES, width), F32),
            pltpu.VMEM((2 * BLOCK, cols, chans), BF),
            pltpu.VMEM((BLOCK * cols, width), BF),
            pltpu.VMEM((9, 8, width), F32),
            pltpu.VMEM((8, width), F32),
            pltpu.VMEM((8, width), F32),
            pltpu.VMEM((2, 2, rows, 128), F32),
            pltpu.VMEM((2, 16 * rows // TILE, 128), F32),
            pltpu.VMEM((BLOCK, 2, cols, 128), F32),
        ],
        compiler_params=pltpu.CompilerParams(vmem_limit_bytes=VMEM),
        cost_estimate=pl.CostEstimate(
            flops=4 * cells * chans * width,
            bytes_accessed=4 * cells * chans,
            transcendentals=2 * cells * width,
        ),
    )(coded, scales, left, right, *arrays, *weights)


def attend_kernel(
    m_ref,
    wq_ref,
    wk_ref,
    wv_ref,
    wo_ref,
    kmask_ref,
    vmask_ref,
    ones_ref,
    out_ref,
    n_ref,
    q_ref,
    k_ref,
    v_ref,
    p_ref,
    a_ref,
    u_ref,
):
    cells, count, chans = m_ref.shape
    total = cells * count
    pairs = HEADS // 2
    m = m_ref[...].astype(F32).reshape(total, chans)
    center = jnp.mean(m, axis=-1, keepdims=True)
    apart = m - center
    spread = jnp.mean(apart * apart, axis=-1, keepdims=True)
    normed = apart * lax.rsqrt(spread + 1e-05)
    for half in range(2):
        n_ref[half] = normed[:, half * 128 : half * 128 + 128]
    qscale = float(HEAD_DIM**-0.5 * 1.4426950408889634)
    tall = jnp.concatenate(
        [
            jnp.concatenate(
                [n_ref[half, pl.ds(g, cells, stride=count), :] for half in range(2)], axis=1
            )
            for g in range(count)
        ],
        axis=0,
    ).astype(BF)
    q_ref[...] = (jnp.dot(tall, wq_ref[...], preferred_element_type=F32) * qscale).astype(BF)
    k_ref[...] = jnp.dot(tall, wk_ref[...], preferred_element_type=F32).astype(BF)
    v_ref[...] = jnp.dot(tall, wv_ref[...], preferred_element_type=F32).astype(BF)

    blank = jnp.zeros((64, 128), BF)
    tall = []
    for g in range(count):
        here = slice(g * cells, (g + 1) * cells)
        k = k_ref[here, :]
        kt = jnp.concatenate([k, k], axis=0).T * kmask_ref[...]
        q = q_ref[here, :]
        parts = []
        for side in range(2):
            lanes = slice(side * 128, side * 128 + 128)
            upper, lower = kt[side * 128 : side * 128 + 64], kt[side * 128 + 64 : side * 128 + 128]
            keys = jnp.concatenate(
                [
                    jnp.concatenate([upper, blank], axis=0),
                    jnp.concatenate([blank, lower], axis=0),
                ],
                axis=1,
            )
            parts.append(jnp.dot(q[:, lanes], keys, preferred_element_type=F32))
        tall.append(jnp.concatenate(parts, axis=1))
    scores = jnp.concatenate(tall, axis=0)
    first = lax.broadcasted_iota(jnp.int32, (1, 128), 1) < 64
    low = jnp.float32(-jnp.inf)
    for pair in range(pairs):
        lanes = slice(pair * 128, pair * 128 + 128)
        two = scores[:, lanes]
        top = jnp.where(
            first,
            jnp.max(jnp.where(first, two, low), axis=-1, keepdims=True),
            jnp.max(jnp.where(first, low, two), axis=-1, keepdims=True),
        )
        p_ref[:, lanes] = jnp.exp2(two - top).astype(BF)
    for g in range(count):
        here = slice(g * cells, (g + 1) * cells)
        for side in range(2):
            lanes = slice(side * 128, side * 128 + 128)
            v = v_ref[here, lanes]
            values = jnp.concatenate(
                [v * vmask_ref[h, :, lanes] for h in range(4 * side, 4 * side + 4)], axis=0
            )
            a_ref[here, lanes] = jnp.dot(
                p_ref[here, side * 256 : side * 256 + 256], values, preferred_element_type=F32
            )
    under = jnp.dot(p_ref[...], ones_ref[...], preferred_element_type=F32)
    attended = (a_ref[...] / under).astype(BF)
    update = jnp.dot(attended, wo_ref[...], preferred_element_type=F32)
    for g in range(count):
        for half in range(2):
            u_ref[half, pl.ds(g, cells, stride=count), :] = update[
                g * cells : (g + 1) * cells, half * 128 : half * 128 + 128
            ]
    for half in range(2):
        out_ref[:, :, half * 128 : half * 128 + 128] = (
            u_ref[half].astype(BF).reshape(cells, count, 128)
        )


def attend_call(moved, wq, wk, wv, wo):
    cells, groups, chans = moved.shape
    count = 16
    total = cells * count
    chan, lane = np.arange(chans), np.arange(128)
    kmask = ((chan[:, None] // HEAD_DIM) % 2 == lane[None, :] // 64).astype(BF)
    head = np.arange(HEADS)
    vmask = np.broadcast_to(
        chan[None, None, :] // HEAD_DIM == head[:, None, None], (HEADS, cells, chans)
    ).astype(BF)
    ones = (chan[None, :] // HEAD_DIM == np.arange(HEADS * cells)[:, None] // cells).astype(BF)

    def whole(array):
        return pl.BlockSpec(array.shape, lambda i, n=array.ndim: (0,) * n)

    return pl.pallas_call(
        attend_kernel,
        grid=(groups // count,),
        out_shape=jax.ShapeDtypeStruct(moved.shape, BF),
        in_specs=[
            pl.BlockSpec((cells, count, chans), lambda i: (0, i, 0)),
            *[whole(a) for a in (wq, wk, wv, wo, kmask, vmask, ones)],
        ],
        out_specs=pl.BlockSpec((cells, count, chans), lambda i: (0, i, 0)),
        scratch_shapes=[
            pltpu.VMEM((2, total, 128), F32),
            pltpu.VMEM((total, chans), BF),
            pltpu.VMEM((total, chans), BF),
            pltpu.VMEM((total, chans), BF),
            pltpu.VMEM((total, HEADS * cells), BF),
            pltpu.VMEM((total, chans), F32),
            pltpu.VMEM((2, total, 128), F32),
        ],
        compiler_params=pltpu.CompilerParams(vmem_limit_bytes=VMEM),
        cost_estimate=pl.CostEstimate(
            flops=2 * cells * groups * chans * (4 * chans + 4 * cells),
            bytes_accessed=4 * cells * groups * chans,
            transcendentals=cells * groups * cells * HEADS,
        ),
    )(moved, wq, wk, wv, wo, kmask, vmask, ones)


def finish_kernel(mixed_ref, home_ref, *refs):
    refs[-1][...] = (mixed_ref[...].astype(F32) + home_ref[...].astype(F32)).astype(BF)


def finish_call(mixed, home, rows, firsts, out):
    block = 16
    blocks = mixed.shape[0] // len(firsts) // block
    stride = (firsts[-1] - firsts[0]) // block
    spec = pl.BlockSpec((block, *mixed.shape[1:]), lambda i: (i, 0, 0))

    def place(i):
        return firsts[0] // block + i // blocks * stride + lax.rem(i, blocks), 0, 0

    held = [] if out is None else [out]
    return pl.pallas_call(
        finish_kernel,
        grid=(mixed.shape[0] // block,),
        out_shape=jax.ShapeDtypeStruct((rows, *mixed.shape[1:]), BF),
        in_specs=[spec, spec, *[pl.BlockSpec(memory_space=pl.ANY) for _ in held]],
        out_specs=pl.BlockSpec(spec.block_shape, place),
        input_output_aliases={2: 0} if held else {},
        compiler_params=pltpu.CompilerParams(vmem_limit_bytes=VMEM),
        cost_estimate=pl.CostEstimate(
            flops=mixed.size, bytes_accessed=6 * mixed.size, transcendentals=0
        ),
    )(mixed, home, *held)


def dequant(line, scales):
    wide = line.astype(F32).reshape(-1, TILE, line.shape[-1]) * scales[:, None, :]
    return wide.astype(BF).reshape(line.shape)


def swap(axis, low, high):
    peers = lax.axis_size(axis)
    up = [(i, i + 1) for i in range(peers - 1)]
    down = [(i + 1, i) for i in range(peers - 1)]
    return lax.ppermute(high, axis, up), lax.ppermute(low, axis, down)


def per_device(
    coded,
    tile_scales,
    expand_weight,
    expand_bias,
    depth_kernel,
    depth_bias,
    project_weight,
    project_bias,
    query_weight,
    key_weight,
    value_weight,
    out_weight,
):
    rows, cols, chans = coded.shape
    first, last = (dequant(coded[:, at], tile_scales[:, at]) for at in (0, -1))
    left, right = swap("gx", first, last)

    def edge(at):
        line = dequant(coded[at], tile_scales[at])
        return jnp.concatenate([left[at][None], line, right[at][None]], axis=0)

    beyond = swap("gy", edge(0), edge(-1))
    wide = lax.axis_size("gx")
    peers = lax.axis_size("gy") * wide
    parity = [[d for d in range(peers) if d % 2 == core] for core in range(2)]

    def exchange(array):
        return lax.all_to_all(array, ("gy", "gx"), 0, 0, tiled=True, axis_index_groups=parity)

    share = (peers // 2, cols * rows // peers, chans)
    parts = [((rows // 4,), rows // 2), ((0, rows * 3 // 4), rows // 4)]
    out = None
    for firsts, count in parts:
        mixed = mb_call(
            coded,
            tile_scales.transpose(1, 0, 2),
            beyond,
            left,
            right,
            expand_weight,
            expand_bias[None, :],
            depth_kernel,
            depth_bias[None, :],
            project_weight,
            project_bias[None, :],
            firsts,
            count,
        )
        if out is None:
            mixed, beyond = lax.optimization_barrier((mixed, beyond))
        moved = exchange(mixed.reshape(share))
        update = attend_call(moved, query_weight, key_weight, value_weight, out_weight)
        home = exchange(update).reshape(mixed.shape)
        out = finish_call(mixed, home, rows, firsts, out)
    return out


def solution(mesh):
    return jax.shard_map(
        per_device,
        mesh=mesh,
        in_specs=(P("gy", "gx", None), P("gy", "gx", None), *[P()] * 10),
        out_specs=P("gy", "gx", None),
        check_vma=False,
    )
```

```python
import functools

import jax
import jax.numpy as jnp
import numpy as np
from jax import lax
from jax.experimental import pallas as pl
from jax.experimental.pallas import tpu as pltpu
from jax.sharding import PartitionSpec as P

HEAD_DIM = 32
HEADS = 8
TILE = 8
LANES = 8
STEP = 12
SLOTS = STEP + 2
PAIRS = STEP // 2
PAD = 112
BLOCK = 8
RING = 3 * BLOCK
VMEM = 63 * 1024 * 1024

A = 0.7978845608028654
B = A * 0.044715
U = B ** (1.0 / 3.0)
BF = jnp.bfloat16
F32 = jnp.float32


def scaled_gelu(y):
    t = jnp.tanh(y * (y * y + A / U))
    return y * t + y


def mb_kernel(plan, coded_ref, scale_ref, left_ref, right_ref, *refs):
    segments, first, stride, outside = plan
    refs = list(refs)
    outer = [[refs.pop(0) for _ in range(2)] for _ in outside]
    we_ref, be_ref, dk_ref, bd_ref, wp_ref, bp_ref, out_ref = refs[:7]
    xs_ref, lhs_ref, e_ref, xk_ref, dp_ref, taps_ref, beu_ref, bdu_ref, lr_ref, sc_ref, line_ref = refs[7:]
    step = pl.program_id(0)
    length = pl.num_programs(0) // segments
    segment, k = step // length, lax.rem(step, length)
    last = length - 1
    start = first + segment * stride
    _, cols, chans = coded_ref.shape
    width = we_ref.shape[1]
    gy, gx = lax.axis_index("gy"), lax.axis_index("gx")
    tall_devs, wide_devs = lax.axis_size("gy"), lax.axis_size("gx")
    halves = [slice(0, 128), slice(128, 256)]

    @pl.when(step == 0)
    def _():
        for dy in range(3):
            left, mid, right = (dk_ref[3 * dy + n : 3 * dy + n + 1, :] * 0.5 for n in range(3))
            sums = (left, (left + mid + right) * 0.5, (left - mid + right) * 0.5, right)
            for n, tap in enumerate(sums):
                taps_ref[4 * dy + n] = jnp.broadcast_to(tap, (8, width))
        beu_ref[...] = jnp.broadcast_to(be_ref[...] * U, (8, width))
        bdu_ref[...] = jnp.broadcast_to(bd_ref[...] * U, (8, width))
        for half, lanes in enumerate(halves):
            for side, ref in enumerate((left_ref, right_ref)):
                lr_ref[side, half] = ref[:, lanes].astype(F32)
            for col in range(cols // TILE):
                sc_ref[half, pl.ds(col, 8, stride=16), :] = scale_ref[col, :, lanes]

    lane = lax.broadcasted_iota(jnp.int32, (8, 256), 0)
    one, nil = jnp.float32(1), jnp.float32(0)
    edge_left = jnp.where((lane > 0) | (gx > 0), one, nil)
    edge_right = jnp.where((lane < 7) | (gx < wide_devs - 1), one, nil)

    def ring(row):
        return lax.rem(row + 1, RING)

    def fill(at, row, coded, beyond):
        for half, lanes in enumerate(halves):
            x = coded[:, lanes].astype(F32)
            if beyond:
                xs_ref[at, half, 7 : 9 + cols, :] = x
                continue
            tile = pl.multiple_of(row // TILE * 16, 16)
            scales = sc_ref[half, pl.ds(tile, cols // TILE), :]
            x = x.reshape(cols // TILE, TILE, 128) * scales[:, None, :]
            xs_ref[at, half, 8 : 8 + cols, :] = x.reshape(cols, 128)
            xs_ref[at, half, 7:8, :] = lr_ref[0, half, pl.ds(row, 1), :]
            xs_ref[at, half, 8 + cols : 9 + cols, :] = lr_ref[1, half, pl.ds(row, 1), :]

    def gather(at, keep):
        slots = [
            jnp.concatenate(
                [xs_ref[at, half, pl.ds(7 + slot, LANES, stride=STEP), :] for half in range(2)],
                axis=1,
            )
            for slot in range(SLOTS)
        ]
        tall = jnp.concatenate(slots, axis=0)
        lhs_ref[pl.ds(at * SLOTS * LANES, SLOTS * LANES), :] = (tall * U).astype(BF)
        if keep is not None:
            xk_ref[lax.rem(keep, 2 * BLOCK)] = tall[LANES : LANES + cols].astype(BF)

    def expand(count, row, scale):
        for part in range(width // 256):
            cut = slice(part * 256, part * 256 + 256)
            pre = jnp.dot(
                lhs_ref[0 : count * SLOTS * LANES, :], we_ref[:, cut], preferred_element_type=F32
            )
            act = scaled_gelu(pre.reshape(count * SLOTS, LANES, 256) + beu_ref[:, cut])
            act = act.reshape(count, SLOTS, LANES, 256)
            if scale is not None:
                act = act * scale
            for at in range(count):
                pos = ring(row + at)
                line = [act[at, slot] for slot in range(SLOTS)]
                line[0], line[-1] = line[0] * edge_left, line[-1] * edge_right
                for pair in range(PAIRS):
                    a, b, c, d = line[2 * pair : 2 * pair + 4]
                    for n, mix in enumerate((a - c, b + c, c - b, b - d)):
                        e_ref[pos, n * PAIRS + pair, :, cut] = mix

    def outer_row(ref, beyond, row, inside):
        fill(0, row, ref[0], beyond)
        gather(0, None)
        expand(1, row, jnp.where(inside, one, nil) if beyond else None)

    def expand_block():
        for at in range(BLOCK):
            row = start + k * BLOCK + at
            fill(at, row, coded_ref[at], False)
            gather(at, row)
        expand(BLOCK, start + k * BLOCK, None)

    def depth_block():
        above = start + (k - 1) * BLOCK
        for part in range(width // 128):
            cut = slice(part * 128, part * 128 + 128)
            taps = [taps_ref[n, :, cut] for n in range(12)]
            for at in range(BLOCK):
                sums = [None, bdu_ref[:, cut], None, None]
                for dy in range(3):
                    pos = ring(above + at + dy - 1)
                    for n in range(4):
                        term = e_ref[pos, n * PAIRS : (n + 1) * PAIRS, :, cut] * taps[4 * dy + n]
                        sums[n] = term if sums[n] is None else sums[n] + term
                act = scaled_gelu(
                    jnp.stack([sums[0] + sums[1] + sums[2], sums[1] - sums[2] - sums[3]], axis=1)
                )
                dp_ref[at * cols : (at + 1) * cols, cut] = act.reshape(cols, 128).astype(BF)
        proj = jnp.dot(dp_ref[...], wp_ref[...], preferred_element_type=F32)
        proj = proj * (0.5 / U) + bp_ref[...]
        for at in range(BLOCK):
            home = xk_ref[lax.rem(above + at, 2 * BLOCK)].astype(F32)
            mixed = home + proj[at * cols : (at + 1) * cols]
            for half, lanes in enumerate(halves):
                for slot in range(STEP):
                    line_ref[at, half, pl.ds(slot, LANES, stride=STEP), :] = mixed[
                        slot * LANES : slot * LANES + LANES, lanes
                    ]
                out_ref[at, :, lanes] = line_ref[at, half].astype(BF)

    for number, (top, bottom) in enumerate(outer):

        @pl.when((segment == number) & (k == 0))
        def _(number=number, top=top):
            outer_row(top, outside[number][0], start - 1, gy > 0)

        @pl.when((segment == number) & (k == last))
        def _(number=number, bottom=bottom):
            outer_row(bottom, outside[number][1], start + last * BLOCK, gy < tall_devs - 1)

    @pl.when(k == 0)
    def _():
        expand_block()

    @pl.when((k > 0) & (k < last))
    def _():
        expand_block()
        depth_block()

    @pl.when(k == last)
    def _():
        depth_block()


def mb_call(coded, scales, rows_beyond, left, right, we, be, dk, bd, wp, bp, firsts, count):
    rows, cols, chans = coded.shape
    width = we.shape[1]
    blocks, segments = count // BLOCK, len(firsts)
    stride = firsts[1] - firsts[0] if segments > 1 else 0
    line = (1, cols, chans)

    def whole(array):
        return pl.BlockSpec(array.shape, lambda i, n=array.ndim: (0,) * n)

    def place(i):
        return i // (blocks + 1), lax.rem(i, blocks + 1)

    def ahead(i):
        segment, k = place(i)
        return (firsts[0] + segment * stride) // BLOCK + jnp.minimum(k, blocks - 1)

    def behind(i):
        segment, k = place(i)
        return segment * blocks + jnp.maximum(k - 1, 0)

    arrays, specs, outside = [], [], []
    for first in firsts:
        outside.append((first == 0, first + count == rows))
        for side, row in enumerate((first - 1, first + count)):
            if outside[-1][side]:
                arrays.append(rows_beyond[side][None])
                specs.append(whole(arrays[-1]))
            else:
                arrays.append(coded)
                specs.append(pl.BlockSpec(line, lambda i, row=row: (row, 0, 0)))
    weights = (we, be, dk, bd, wp, bp)
    cells = count * segments * cols
    return pl.pallas_call(
        functools.partial(mb_kernel, (segments, firsts[0], stride, tuple(outside))),
        grid=(segments * (blocks + 1),),
        out_shape=jax.ShapeDtypeStruct((segments * count, cols, chans), BF),
        in_specs=[
            pl.BlockSpec((BLOCK, cols, chans), lambda i: (ahead(i), 0, 0)),
            whole(scales),
            whole(left),
            whole(right),
            *specs,
            *[whole(a) for a in weights],
        ],
        out_specs=pl.BlockSpec((BLOCK, cols, chans), lambda i: (behind(i), 0, 0)),
        scratch_shapes=[
            pltpu.VMEM((BLOCK, 2, PAD, 128), F32),
            pltpu.VMEM((BLOCK * SLOTS * LANES, chans), BF),
            pltpu.VMEM((RING, 4 * PAIRS, LANES, width), F32),
            pltpu.VMEM((2 * BLOCK, cols, chans), BF),
            pltpu.VMEM((BLOCK * cols, width), BF),
            pltpu.VMEM((12, 8, width), F32),
            pltpu.VMEM((8, width), F32),
            pltpu.VMEM((8, width), F32),
            pltpu.VMEM((2, 2, rows, 128), F32),
            pltpu.VMEM((2, 16 * rows // TILE, 128), F32),
            pltpu.VMEM((BLOCK, 2, cols, 128), F32),
        ],
        compiler_params=pltpu.CompilerParams(vmem_limit_bytes=VMEM),
        cost_estimate=pl.CostEstimate(
            flops=4 * cells * chans * width,
            bytes_accessed=4 * cells * chans,
            transcendentals=2 * cells * width,
        ),
    )(coded, scales, left, right, *arrays, *weights)


def attend_kernel(
    m_ref,
    wq_ref,
    wk_ref,
    wv_ref,
    wo_ref,
    kmask_ref,
    vmask_ref,
    ones_ref,
    out_ref,
    n_ref,
    q_ref,
    k_ref,
    v_ref,
    p_ref,
    a_ref,
    u_ref,
):
    cells, count, chans = m_ref.shape
    total = cells * count
    pairs = HEADS // 2
    m = m_ref[...].astype(F32).reshape(total, chans)
    center = jnp.mean(m, axis=-1, keepdims=True)
    apart = m - center
    spread = jnp.mean(apart * apart, axis=-1, keepdims=True)
    normed = apart * lax.rsqrt(spread + 1e-05)
    for half in range(2):
        n_ref[half] = normed[:, half * 128 : half * 128 + 128]
    qscale = float(HEAD_DIM**-0.5 * 1.4426950408889634)
    tall = jnp.concatenate(
        [
            jnp.concatenate(
                [n_ref[half, pl.ds(g, cells, stride=count), :] for half in range(2)], axis=1
            )
            for g in range(count)
        ],
        axis=0,
    ).astype(BF)
    q_ref[...] = (jnp.dot(tall, wq_ref[...], preferred_element_type=F32) * qscale).astype(BF)
    k_ref[...] = jnp.dot(tall, wk_ref[...], preferred_element_type=F32).astype(BF)
    v_ref[...] = jnp.dot(tall, wv_ref[...], preferred_element_type=F32).astype(BF)

    blank = jnp.zeros((64, 128), BF)
    tall = []
    for g in range(count):
        here = slice(g * cells, (g + 1) * cells)
        k = k_ref[here, :]
        kt = jnp.concatenate([k, k], axis=0).T * kmask_ref[...]
        q = q_ref[here, :]
        parts = []
        for side in range(2):
            lanes = slice(side * 128, side * 128 + 128)
            upper, lower = kt[side * 128 : side * 128 + 64], kt[side * 128 + 64 : side * 128 + 128]
            keys = jnp.concatenate(
                [
                    jnp.concatenate([upper, blank], axis=0),
                    jnp.concatenate([blank, lower], axis=0),
                ],
                axis=1,
            )
            parts.append(jnp.dot(q[:, lanes], keys, preferred_element_type=F32))
        tall.append(jnp.concatenate(parts, axis=1))
    scores = jnp.concatenate(tall, axis=0)
    first = lax.broadcasted_iota(jnp.int32, (1, 128), 1) < 64
    low = jnp.float32(-jnp.inf)
    for pair in range(pairs):
        lanes = slice(pair * 128, pair * 128 + 128)
        two = scores[:, lanes]
        top = jnp.where(
            first,
            jnp.max(jnp.where(first, two, low), axis=-1, keepdims=True),
            jnp.max(jnp.where(first, low, two), axis=-1, keepdims=True),
        )
        p_ref[:, lanes] = jnp.exp2(two - top).astype(BF)
    for g in range(count):
        here = slice(g * cells, (g + 1) * cells)
        for side in range(2):
            lanes = slice(side * 128, side * 128 + 128)
            v = v_ref[here, lanes]
            values = jnp.concatenate(
                [v * vmask_ref[h, :, lanes] for h in range(4 * side, 4 * side + 4)], axis=0
            )
            a_ref[here, lanes] = jnp.dot(
                p_ref[here, side * 256 : side * 256 + 256], values, preferred_element_type=F32
            )
    under = jnp.dot(p_ref[...], ones_ref[...], preferred_element_type=F32)
    attended = (a_ref[...] / under).astype(BF)
    update = jnp.dot(attended, wo_ref[...], preferred_element_type=F32)
    for g in range(count):
        for half in range(2):
            u_ref[half, pl.ds(g, cells, stride=count), :] = update[
                g * cells : (g + 1) * cells, half * 128 : half * 128 + 128
            ]
    for half in range(2):
        out_ref[:, :, half * 128 : half * 128 + 128] = (
            u_ref[half].astype(BF).reshape(cells, count, 128)
        )


def attend_call(moved, wq, wk, wv, wo):
    cells, groups, chans = moved.shape
    count = 16
    total = cells * count
    chan, lane = np.arange(chans), np.arange(128)
    kmask = ((chan[:, None] // HEAD_DIM) % 2 == lane[None, :] // 64).astype(BF)
    head = np.arange(HEADS)
    vmask = np.broadcast_to(
        chan[None, None, :] // HEAD_DIM == head[:, None, None], (HEADS, cells, chans)
    ).astype(BF)
    ones = (chan[None, :] // HEAD_DIM == np.arange(HEADS * cells)[:, None] // cells).astype(BF)

    def whole(array):
        return pl.BlockSpec(array.shape, lambda i, n=array.ndim: (0,) * n)

    return pl.pallas_call(
        attend_kernel,
        grid=(groups // count,),
        out_shape=jax.ShapeDtypeStruct(moved.shape, BF),
        in_specs=[
            pl.BlockSpec((cells, count, chans), lambda i: (0, i, 0)),
            *[whole(a) for a in (wq, wk, wv, wo, kmask, vmask, ones)],
        ],
        out_specs=pl.BlockSpec((cells, count, chans), lambda i: (0, i, 0)),
        scratch_shapes=[
            pltpu.VMEM((2, total, 128), F32),
            pltpu.VMEM((total, chans), BF),
            pltpu.VMEM((total, chans), BF),
            pltpu.VMEM((total, chans), BF),
            pltpu.VMEM((total, HEADS * cells), BF),
            pltpu.VMEM((total, chans), F32),
            pltpu.VMEM((2, total, 128), F32),
        ],
        compiler_params=pltpu.CompilerParams(vmem_limit_bytes=VMEM),
        cost_estimate=pl.CostEstimate(
            flops=2 * cells * groups * chans * (4 * chans + 4 * cells),
            bytes_accessed=4 * cells * groups * chans,
            transcendentals=cells * groups * cells * HEADS,
        ),
    )(moved, wq, wk, wv, wo, kmask, vmask, ones)


def finish_kernel(mixed_ref, home_ref, *refs):
    refs[-1][...] = (mixed_ref[...].astype(F32) + home_ref[...].astype(F32)).astype(BF)


def finish_call(mixed, home, rows, firsts, out):
    block = 16
    blocks = mixed.shape[0] // len(firsts) // block
    stride = (firsts[-1] - firsts[0]) // block
    spec = pl.BlockSpec((block, *mixed.shape[1:]), lambda i: (i, 0, 0))

    def place(i):
        return firsts[0] // block + i // blocks * stride + lax.rem(i, blocks), 0, 0

    held = [] if out is None else [out]
    return pl.pallas_call(
        finish_kernel,
        grid=(mixed.shape[0] // block,),
        out_shape=jax.ShapeDtypeStruct((rows, *mixed.shape[1:]), BF),
        in_specs=[spec, spec, *[pl.BlockSpec(memory_space=pl.ANY) for _ in held]],
        out_specs=pl.BlockSpec(spec.block_shape, place),
        input_output_aliases={2: 0} if held else {},
        compiler_params=pltpu.CompilerParams(vmem_limit_bytes=VMEM),
        cost_estimate=pl.CostEstimate(
            flops=mixed.size, bytes_accessed=6 * mixed.size, transcendentals=0
        ),
    )(mixed, home, *held)


def dequant(line, scales):
    wide = line.astype(F32).reshape(-1, TILE, line.shape[-1]) * scales[:, None, :]
    return wide.astype(BF).reshape(line.shape)


def swap(axis, low, high):
    peers = lax.axis_size(axis)
    up = [(i, i + 1) for i in range(peers - 1)]
    down = [(i + 1, i) for i in range(peers - 1)]
    return lax.ppermute(high, axis, up), lax.ppermute(low, axis, down)


def per_device(
    coded,
    tile_scales,
    expand_weight,
    expand_bias,
    depth_kernel,
    depth_bias,
    project_weight,
    project_bias,
    query_weight,
    key_weight,
    value_weight,
    out_weight,
):
    rows, cols, chans = coded.shape
    first, last = (dequant(coded[:, at], tile_scales[:, at]) for at in (0, -1))
    left, right = swap("gx", first, last)

    def edge(at):
        line = dequant(coded[at], tile_scales[at])
        return jnp.concatenate([left[at][None], line, right[at][None]], axis=0)

    beyond = swap("gy", edge(0), edge(-1))
    wide = lax.axis_size("gx")
    peers = lax.axis_size("gy") * wide
    parity = [[d for d in range(peers) if d % 2 == core] for core in range(2)]

    def exchange(array):
        return lax.all_to_all(array, ("gy", "gx"), 0, 0, tiled=True, axis_index_groups=parity)

    share = (peers // 2, cols * rows // peers, chans)
    parts = [((rows // 4,), rows // 2), ((0, rows * 3 // 4), rows // 4)]
    out = None
    for firsts, count in parts:
        mixed = mb_call(
            coded,
            tile_scales.transpose(1, 0, 2),
            beyond,
            left,
            right,
            expand_weight,
            expand_bias[None, :],
            depth_kernel,
            depth_bias[None, :],
            project_weight,
            project_bias[None, :],
            firsts,
            count,
        )
        if out is None:
            mixed, beyond = lax.optimization_barrier((mixed, beyond))
        moved = exchange(mixed.reshape(share))
        update = attend_call(moved, query_weight, key_weight, value_weight, out_weight)
        home = exchange(update).reshape(mixed.shape)
        if out is None:
            out = finish_call(mixed, home, rows, firsts, out)
            continue
        for number, first in enumerate(firsts):
            here = slice(number * count, (number + 1) * count)
            piece = (mixed[here].astype(F32) + home[here].astype(F32)).astype(BF)
            out = lax.dynamic_update_slice(out, piece, (first, 0, 0))
    return out


def solution(mesh):
    return jax.shard_map(
        per_device,
        mesh=mesh,
        in_specs=(P("gy", "gx", None), P("gy", "gx", None), *[P()] * 10),
        out_specs=P("gy", "gx", None),
        check_vma=False,
    )
```

```python
import functools

import jax
import jax.numpy as jnp
import numpy as np
from jax import lax
from jax.experimental import pallas as pl
from jax.experimental.pallas import tpu as pltpu
from jax.sharding import PartitionSpec as P

HEAD_DIM = 32
HEADS = 8
TILE = 8
LANES = 8
STEP = 12
SLOTS = STEP + 2
PAIRS = STEP // 2
PAD = 112
BLOCK = 8
RING = 3 * BLOCK
VMEM = 63 * 1024 * 1024

A = 0.7978845608028654
B = A * 0.044715
U = B ** (1.0 / 3.0)
BF = jnp.bfloat16
F32 = jnp.float32


def scaled_gelu(y):
    t = jnp.tanh(y * (y * y + A / U))
    return y * t + y


def mb_kernel(plan, coded_ref, scale_ref, left_ref, right_ref, *refs):
    segments, first, stride, outside = plan
    refs = list(refs)
    outer = [[refs.pop(0) for _ in range(2)] for _ in outside]
    we_ref, be_ref, dk_ref, bd_ref, wp_ref, bp_ref, out_ref = refs[:7]
    xs_ref, lhs_ref, e_ref, xk_ref, dp_ref, taps_ref, beu_ref, bdu_ref, lr_ref, sc_ref, line_ref = refs[7:]
    step = pl.program_id(0)
    length = pl.num_programs(0) // segments
    segment, k = step // length, lax.rem(step, length)
    last = length - 1
    start = first + segment * stride
    _, cols, chans = coded_ref.shape
    width = we_ref.shape[1]
    gy, gx = lax.axis_index("gy"), lax.axis_index("gx")
    tall_devs, wide_devs = lax.axis_size("gy"), lax.axis_size("gx")
    halves = [slice(0, 128), slice(128, 256)]

    @pl.when(step == 0)
    def _():
        for dy in range(3):
            left, mid, right = (dk_ref[3 * dy + n : 3 * dy + n + 1, :] * 0.5 for n in range(3))
            sums = (left, (left + mid + right) * 0.5, (left - mid + right) * 0.5, right)
            for n, tap in enumerate(sums):
                taps_ref[4 * dy + n] = jnp.broadcast_to(tap, (8, width))
        beu_ref[...] = jnp.broadcast_to(be_ref[...] * U, (8, width))
        bdu_ref[...] = jnp.broadcast_to(bd_ref[...] * U, (8, width))
        for half, lanes in enumerate(halves):
            for side, ref in enumerate((left_ref, right_ref)):
                lr_ref[side, half] = ref[:, lanes].astype(F32)
            for col in range(cols // TILE):
                sc_ref[half, pl.ds(col, 8, stride=16), :] = scale_ref[col, :, lanes]

    lane = lax.broadcasted_iota(jnp.int32, (8, 256), 0)
    one, nil = jnp.float32(1), jnp.float32(0)
    edge_left = jnp.where((lane > 0) | (gx > 0), one, nil)
    edge_right = jnp.where((lane < 7) | (gx < wide_devs - 1), one, nil)

    def ring(row):
        return lax.rem(row + 1, RING)

    def fill(at, row, coded, beyond):
        for half, lanes in enumerate(halves):
            x = coded[:, lanes].astype(F32)
            if beyond:
                xs_ref[at, half, 7 : 9 + cols, :] = x
                continue
            tile = pl.multiple_of(row // TILE * 16, 16)
            scales = sc_ref[half, pl.ds(tile, cols // TILE), :]
            x = x.reshape(cols // TILE, TILE, 128) * scales[:, None, :]
            xs_ref[at, half, 8 : 8 + cols, :] = x.reshape(cols, 128)
            xs_ref[at, half, 7:8, :] = lr_ref[0, half, pl.ds(row, 1), :]
            xs_ref[at, half, 8 + cols : 9 + cols, :] = lr_ref[1, half, pl.ds(row, 1), :]

    def gather(at, keep):
        slots = [
            jnp.concatenate(
                [xs_ref[at, half, pl.ds(7 + slot, LANES, stride=STEP), :] for half in range(2)],
                axis=1,
            )
            for slot in range(SLOTS)
        ]
        tall = jnp.concatenate(slots, axis=0)
        lhs_ref[pl.ds(at * SLOTS * LANES, SLOTS * LANES), :] = (tall * U).astype(BF)
        if keep is not None:
            xk_ref[lax.rem(keep, 2 * BLOCK)] = tall[LANES : LANES + cols].astype(BF)

    def expand(count, row, scale):
        for part in range(width // 256):
            cut = slice(part * 256, part * 256 + 256)
            pre = jnp.dot(
                lhs_ref[0 : count * SLOTS * LANES, :], we_ref[:, cut], preferred_element_type=F32
            )
            act = scaled_gelu(pre.reshape(count * SLOTS, LANES, 256) + beu_ref[:, cut])
            act = act.reshape(count, SLOTS, LANES, 256)
            if scale is not None:
                act = act * scale
            for at in range(count):
                pos = ring(row + at)
                line = [act[at, slot] for slot in range(SLOTS)]
                line[0], line[-1] = line[0] * edge_left, line[-1] * edge_right
                for pair in range(PAIRS):
                    a, b, c, d = line[2 * pair : 2 * pair + 4]
                    for n, mix in enumerate((a - c, b + c, c - b, b - d)):
                        e_ref[pos, n * PAIRS + pair, :, cut] = mix

    def outer_row(ref, beyond, row, inside):
        fill(0, row, ref[0], beyond)
        gather(0, None)
        expand(1, row, jnp.where(inside, one, nil) if beyond else None)

    def expand_block():
        for at in range(BLOCK):
            row = start + k * BLOCK + at
            fill(at, row, coded_ref[at], False)
            gather(at, row)
        expand(BLOCK, start + k * BLOCK, None)

    def depth_block():
        above = start + (k - 1) * BLOCK
        for part in range(width // 128):
            cut = slice(part * 128, part * 128 + 128)
            taps = [taps_ref[n, :, cut] for n in range(12)]
            for at in range(BLOCK):
                sums = [None, bdu_ref[:, cut], None, None]
                for dy in range(3):
                    pos = ring(above + at + dy - 1)
                    for n in range(4):
                        term = e_ref[pos, n * PAIRS : (n + 1) * PAIRS, :, cut] * taps[4 * dy + n]
                        sums[n] = term if sums[n] is None else sums[n] + term
                act = scaled_gelu(
                    jnp.stack([sums[0] + sums[1] + sums[2], sums[1] - sums[2] - sums[3]], axis=1)
                )
                dp_ref[at * cols : (at + 1) * cols, cut] = act.reshape(cols, 128).astype(BF)
        proj = jnp.dot(dp_ref[...], wp_ref[...], preferred_element_type=F32)
        proj = proj * (0.5 / U) + bp_ref[...]
        for at in range(BLOCK):
            home = xk_ref[lax.rem(above + at, 2 * BLOCK)].astype(F32)
            mixed = home + proj[at * cols : (at + 1) * cols]
            for half, lanes in enumerate(halves):
                for slot in range(STEP):
                    line_ref[at, half, pl.ds(slot, LANES, stride=STEP), :] = mixed[
                        slot * LANES : slot * LANES + LANES, lanes
                    ]
                out_ref[at, :, lanes] = line_ref[at, half].astype(BF)

    for number, (top, bottom) in enumerate(outer):

        @pl.when((segment == number) & (k == 0))
        def _(number=number, top=top):
            outer_row(top, outside[number][0], start - 1, gy > 0)

        @pl.when((segment == number) & (k == last))
        def _(number=number, bottom=bottom):
            outer_row(bottom, outside[number][1], start + last * BLOCK, gy < tall_devs - 1)

    @pl.when(k == 0)
    def _():
        expand_block()

    @pl.when((k > 0) & (k < last))
    def _():
        expand_block()
        depth_block()

    @pl.when(k == last)
    def _():
        depth_block()


def mb_call(coded, scales, rows_beyond, left, right, we, be, dk, bd, wp, bp, firsts, count):
    rows, cols, chans = coded.shape
    width = we.shape[1]
    blocks, segments = count // BLOCK, len(firsts)
    stride = firsts[1] - firsts[0] if segments > 1 else 0
    line = (1, cols, chans)

    def whole(array):
        return pl.BlockSpec(array.shape, lambda i, n=array.ndim: (0,) * n)

    def place(i):
        return i // (blocks + 1), lax.rem(i, blocks + 1)

    def ahead(i):
        segment, k = place(i)
        return (firsts[0] + segment * stride) // BLOCK + jnp.minimum(k, blocks - 1)

    def behind(i):
        segment, k = place(i)
        return segment * blocks + jnp.maximum(k - 1, 0)

    arrays, specs, outside = [], [], []
    for first in firsts:
        outside.append((first == 0, first + count == rows))
        for side, row in enumerate((first - 1, first + count)):
            if outside[-1][side]:
                arrays.append(rows_beyond[side][None])
                specs.append(whole(arrays[-1]))
            else:
                arrays.append(coded)
                specs.append(pl.BlockSpec(line, lambda i, row=row: (row, 0, 0)))
    weights = (we, be, dk, bd, wp, bp)
    cells = count * segments * cols
    return pl.pallas_call(
        functools.partial(mb_kernel, (segments, firsts[0], stride, tuple(outside))),
        grid=(segments * (blocks + 1),),
        out_shape=jax.ShapeDtypeStruct((segments * count, cols, chans), BF),
        in_specs=[
            pl.BlockSpec((BLOCK, cols, chans), lambda i: (ahead(i), 0, 0)),
            whole(scales),
            whole(left),
            whole(right),
            *specs,
            *[whole(a) for a in weights],
        ],
        out_specs=pl.BlockSpec((BLOCK, cols, chans), lambda i: (behind(i), 0, 0)),
        scratch_shapes=[
            pltpu.VMEM((BLOCK, 2, PAD, 128), F32),
            pltpu.VMEM((BLOCK * SLOTS * LANES, chans), BF),
            pltpu.VMEM((RING, 4 * PAIRS, LANES, width), F32),
            pltpu.VMEM((2 * BLOCK, cols, chans), BF),
            pltpu.VMEM((BLOCK * cols, width), BF),
            pltpu.VMEM((12, 8, width), F32),
            pltpu.VMEM((8, width), F32),
            pltpu.VMEM((8, width), F32),
            pltpu.VMEM((2, 2, rows, 128), F32),
            pltpu.VMEM((2, 16 * rows // TILE, 128), F32),
            pltpu.VMEM((BLOCK, 2, cols, 128), F32),
        ],
        compiler_params=pltpu.CompilerParams(vmem_limit_bytes=VMEM),
        cost_estimate=pl.CostEstimate(
            flops=4 * cells * chans * width,
            bytes_accessed=4 * cells * chans,
            transcendentals=2 * cells * width,
        ),
    )(coded, scales, left, right, *arrays, *weights)


def attend_kernel(
    m_ref,
    wq_ref,
    wk_ref,
    wv_ref,
    wo_ref,
    kmask_ref,
    vmask_ref,
    ones_ref,
    out_ref,
    n_ref,
    q_ref,
    k_ref,
    v_ref,
    p_ref,
    a_ref,
    u_ref,
):
    cells, count, chans = m_ref.shape
    total = cells * count
    pairs = HEADS // 2
    m = m_ref[...].astype(F32).reshape(total, chans)
    center = jnp.mean(m, axis=-1, keepdims=True)
    apart = m - center
    spread = jnp.mean(apart * apart, axis=-1, keepdims=True)
    normed = apart * lax.rsqrt(spread + 1e-05)
    for half in range(2):
        n_ref[half] = normed[:, half * 128 : half * 128 + 128]
    qscale = float(HEAD_DIM**-0.5 * 1.4426950408889634)
    tall = jnp.concatenate(
        [
            jnp.concatenate(
                [n_ref[half, pl.ds(g, cells, stride=count), :] for half in range(2)], axis=1
            )
            for g in range(count)
        ],
        axis=0,
    ).astype(BF)
    q_ref[...] = (jnp.dot(tall, wq_ref[...], preferred_element_type=F32) * qscale).astype(BF)
    k_ref[...] = jnp.dot(tall, wk_ref[...], preferred_element_type=F32).astype(BF)
    v_ref[...] = jnp.dot(tall, wv_ref[...], preferred_element_type=F32).astype(BF)

    blank = jnp.zeros((64, 128), BF)
    tall = []
    for g in range(count):
        here = slice(g * cells, (g + 1) * cells)
        k = k_ref[here, :]
        kt = jnp.concatenate([k, k], axis=0).T * kmask_ref[...]
        q = q_ref[here, :]
        parts = []
        for side in range(2):
            lanes = slice(side * 128, side * 128 + 128)
            upper, lower = kt[side * 128 : side * 128 + 64], kt[side * 128 + 64 : side * 128 + 128]
            keys = jnp.concatenate(
                [
                    jnp.concatenate([upper, blank], axis=0),
                    jnp.concatenate([blank, lower], axis=0),
                ],
                axis=1,
            )
            parts.append(jnp.dot(q[:, lanes], keys, preferred_element_type=F32))
        tall.append(jnp.concatenate(parts, axis=1))
    scores = jnp.concatenate(tall, axis=0)
    first = lax.broadcasted_iota(jnp.int32, (1, 128), 1) < 64
    low = jnp.float32(-jnp.inf)
    for pair in range(pairs):
        lanes = slice(pair * 128, pair * 128 + 128)
        two = scores[:, lanes]
        top = jnp.where(
            first,
            jnp.max(jnp.where(first, two, low), axis=-1, keepdims=True),
            jnp.max(jnp.where(first, low, two), axis=-1, keepdims=True),
        )
        p_ref[:, lanes] = jnp.exp2(two - top).astype(BF)
    for g in range(count):
        here = slice(g * cells, (g + 1) * cells)
        for side in range(2):
            lanes = slice(side * 128, side * 128 + 128)
            v = v_ref[here, lanes]
            values = jnp.concatenate(
                [v * vmask_ref[h, :, lanes] for h in range(4 * side, 4 * side + 4)], axis=0
            )
            a_ref[here, lanes] = jnp.dot(
                p_ref[here, side * 256 : side * 256 + 256], values, preferred_element_type=F32
            )
    under = jnp.dot(p_ref[...], ones_ref[...], preferred_element_type=F32)
    attended = (a_ref[...] / under).astype(BF)
    update = jnp.dot(attended, wo_ref[...], preferred_element_type=F32)
    for g in range(count):
        for half in range(2):
            u_ref[half, pl.ds(g, cells, stride=count), :] = update[
                g * cells : (g + 1) * cells, half * 128 : half * 128 + 128
            ]
    for half in range(2):
        out_ref[:, :, half * 128 : half * 128 + 128] = (
            u_ref[half].astype(BF).reshape(cells, count, 128)
        )


def attend_call(moved, wq, wk, wv, wo):
    cells, groups, chans = moved.shape
    count = 16
    total = cells * count
    chan, lane = np.arange(chans), np.arange(128)
    kmask = ((chan[:, None] // HEAD_DIM) % 2 == lane[None, :] // 64).astype(BF)
    head = np.arange(HEADS)
    vmask = np.broadcast_to(
        chan[None, None, :] // HEAD_DIM == head[:, None, None], (HEADS, cells, chans)
    ).astype(BF)
    ones = (chan[None, :] // HEAD_DIM == np.arange(HEADS * cells)[:, None] // cells).astype(BF)

    def whole(array):
        return pl.BlockSpec(array.shape, lambda i, n=array.ndim: (0,) * n)

    return pl.pallas_call(
        attend_kernel,
        grid=(groups // count,),
        out_shape=jax.ShapeDtypeStruct(moved.shape, BF),
        in_specs=[
            pl.BlockSpec((cells, count, chans), lambda i: (0, i, 0)),
            *[whole(a) for a in (wq, wk, wv, wo, kmask, vmask, ones)],
        ],
        out_specs=pl.BlockSpec((cells, count, chans), lambda i: (0, i, 0)),
        scratch_shapes=[
            pltpu.VMEM((2, total, 128), F32),
            pltpu.VMEM((total, chans), BF),
            pltpu.VMEM((total, chans), BF),
            pltpu.VMEM((total, chans), BF),
            pltpu.VMEM((total, HEADS * cells), BF),
            pltpu.VMEM((total, chans), F32),
            pltpu.VMEM((2, total, 128), F32),
        ],
        compiler_params=pltpu.CompilerParams(vmem_limit_bytes=VMEM),
        cost_estimate=pl.CostEstimate(
            flops=2 * cells * groups * chans * (4 * chans + 4 * cells),
            bytes_accessed=4 * cells * groups * chans,
            transcendentals=cells * groups * cells * HEADS,
        ),
    )(moved, wq, wk, wv, wo, kmask, vmask, ones)


def finish_kernel(mixed_ref, home_ref, *refs):
    refs[-1][...] = (mixed_ref[...].astype(F32) + home_ref[...].astype(F32)).astype(BF)


def finish_call(mixed, home, rows, firsts, out):
    block = 16
    blocks = mixed.shape[0] // len(firsts) // block
    stride = (firsts[-1] - firsts[0]) // block
    spec = pl.BlockSpec((block, *mixed.shape[1:]), lambda i: (i, 0, 0))

    def place(i):
        return firsts[0] // block + i // blocks * stride + lax.rem(i, blocks), 0, 0

    held = [] if out is None else [out]
    return pl.pallas_call(
        finish_kernel,
        grid=(mixed.shape[0] // block,),
        out_shape=jax.ShapeDtypeStruct((rows, *mixed.shape[1:]), BF),
        in_specs=[spec, spec, *[pl.BlockSpec(memory_space=pl.ANY) for _ in held]],
        out_specs=pl.BlockSpec(spec.block_shape, place),
        input_output_aliases={2: 0} if held else {},
        compiler_params=pltpu.CompilerParams(vmem_limit_bytes=VMEM),
        cost_estimate=pl.CostEstimate(
            flops=mixed.size, bytes_accessed=6 * mixed.size, transcendentals=0
        ),
    )(mixed, home, *held)


def dequant(line, scales):
    wide = line.astype(F32).reshape(-1, TILE, line.shape[-1]) * scales[:, None, :]
    return wide.astype(BF).reshape(line.shape)


def swap(axis, low, high):
    peers = lax.axis_size(axis)
    up = [(i, i + 1) for i in range(peers - 1)]
    down = [(i + 1, i) for i in range(peers - 1)]
    return lax.ppermute(high, axis, up), lax.ppermute(low, axis, down)


def per_device(
    coded,
    tile_scales,
    expand_weight,
    expand_bias,
    depth_kernel,
    depth_bias,
    project_weight,
    project_bias,
    query_weight,
    key_weight,
    value_weight,
    out_weight,
):
    rows, cols, chans = coded.shape
    first, last = (dequant(coded[:, at], tile_scales[:, at]) for at in (0, -1))
    left, right = swap("gx", first, last)

    def edge(at):
        line = dequant(coded[at], tile_scales[at])
        return jnp.concatenate([left[at][None], line, right[at][None]], axis=0)

    beyond = swap("gy", edge(0), edge(-1))
    wide = lax.axis_size("gx")
    peers = lax.axis_size("gy") * wide
    parity = [[d for d in range(peers) if d % 2 == core] for core in range(2)]

    def exchange(array):
        return lax.all_to_all(array, ("gy", "gx"), 0, 0, tiled=True, axis_index_groups=parity)

    share = (peers // 2, cols * rows // peers, chans)
    parts = [((rows // 4,), rows // 2), ((0, rows * 3 // 4), rows // 4)]
    out = None
    for firsts, count in parts:
        mixed = mb_call(
            coded,
            tile_scales.transpose(1, 0, 2),
            beyond,
            left,
            right,
            expand_weight,
            expand_bias[None, :],
            depth_kernel,
            depth_bias[None, :],
            project_weight,
            project_bias[None, :],
            firsts,
            count,
        )
        if out is None:
            mixed, beyond = lax.optimization_barrier((mixed, beyond))
        moved = exchange(mixed.reshape(share))
        update = attend_call(moved, query_weight, key_weight, value_weight, out_weight)
        home = exchange(update).reshape(mixed.shape)
        out = finish_call(mixed, home, rows, firsts, out)
    return out


def solution(mesh):
    return jax.shard_map(
        per_device,
        mesh=mesh,
        in_specs=(P("gy", "gx", None), P("gy", "gx", None), *[P()] * 10),
        out_specs=P("gy", "gx", None),
        check_vma=False,
    )
```

```python
import functools

import jax
import jax.numpy as jnp
import numpy as np
from jax import lax
from jax.experimental import pallas as pl
from jax.experimental.pallas import tpu as pltpu
from jax.sharding import PartitionSpec as P

HEAD_DIM = 32
HEADS = 8
TILE = 8
LANES = 8
STEP = 12
SLOTS = STEP + 2
PAIRS = STEP // 2
PAD = 112
BLOCK = 8
RING = 3 * BLOCK
VMEM = 63 * 1024 * 1024

A = 0.7978845608028654
B = A * 0.044715
U = B ** (1.0 / 3.0)
BF = jnp.bfloat16
F32 = jnp.float32


def scaled_gelu(y):
    t = jnp.tanh(y * (y * y + A / U))
    return y * t + y


def mb_kernel(plan, coded_ref, scale_ref, left_ref, right_ref, *refs):
    segments, first, stride, outside = plan
    refs = list(refs)
    outer = [[refs.pop(0) for _ in range(2)] for _ in outside]
    we_ref, be_ref, dk_ref, bd_ref, wp_ref, bp_ref, out_ref = refs[:7]
    xs_ref, lhs_ref, e_ref, xk_ref, dp_ref, taps_ref, beu_ref, bdu_ref, lr_ref, sc_ref, line_ref = refs[7:]
    step = pl.program_id(0)
    length = pl.num_programs(0) // segments
    segment, k = step // length, lax.rem(step, length)
    last = length - 1
    start = first + segment * stride
    _, cols, chans = coded_ref.shape
    width = we_ref.shape[1]
    gy, gx = lax.axis_index("gy"), lax.axis_index("gx")
    tall_devs, wide_devs = lax.axis_size("gy"), lax.axis_size("gx")
    halves = [slice(0, 128), slice(128, 256)]

    @pl.when(step == 0)
    def _():
        for dy in range(3):
            left, mid, right = (dk_ref[3 * dy + n : 3 * dy + n + 1, :] * 0.5 for n in range(3))
            sums = (left, (left + mid + right) * 0.5, (left - mid + right) * 0.5, right)
            for n, tap in enumerate(sums):
                taps_ref[4 * dy + n] = jnp.broadcast_to(tap, (8, width))
        beu_ref[...] = jnp.broadcast_to(be_ref[...] * U, (8, width))
        bdu_ref[...] = jnp.broadcast_to(bd_ref[...] * U, (8, width))
        for half, lanes in enumerate(halves):
            for side, ref in enumerate((left_ref, right_ref)):
                lr_ref[side, half] = ref[:, lanes].astype(F32)
            for col in range(cols // TILE):
                sc_ref[half, pl.ds(col, 8, stride=16), :] = scale_ref[col, :, lanes]

    lane = lax.broadcasted_iota(jnp.int32, (8, 256), 0)
    one, nil = jnp.float32(1), jnp.float32(0)
    edge_left = jnp.where((lane > 0) | (gx > 0), one, nil)
    edge_right = jnp.where((lane < 7) | (gx < wide_devs - 1), one, nil)

    def ring(row):
        return lax.rem(row + 1, RING)

    def fill(at, row, coded, beyond):
        for half, lanes in enumerate(halves):
            x = coded[:, lanes].astype(F32)
            if beyond:
                xs_ref[at, half, 7 : 9 + cols, :] = x
                continue
            tile = pl.multiple_of(row // TILE * 16, 16)
            scales = sc_ref[half, pl.ds(tile, cols // TILE), :]
            x = x.reshape(cols // TILE, TILE, 128) * scales[:, None, :]
            xs_ref[at, half, 8 : 8 + cols, :] = x.reshape(cols, 128)
            xs_ref[at, half, 7:8, :] = lr_ref[0, half, pl.ds(row, 1), :]
            xs_ref[at, half, 8 + cols : 9 + cols, :] = lr_ref[1, half, pl.ds(row, 1), :]

    def gather(at, keep):
        slots = [
            jnp.concatenate(
                [xs_ref[at, half, pl.ds(7 + slot, LANES, stride=STEP), :] for half in range(2)],
                axis=1,
            )
            for slot in range(SLOTS)
        ]
        tall = jnp.concatenate(slots, axis=0)
        lhs_ref[pl.ds(at * SLOTS * LANES, SLOTS * LANES), :] = (tall * U).astype(BF)
        if keep is not None:
            xk_ref[lax.rem(keep, 2 * BLOCK)] = tall[LANES : LANES + cols].astype(BF)

    def expand(count, row, scale):
        for part in range(width // 256):
            cut = slice(part * 256, part * 256 + 256)
            pre = jnp.dot(
                lhs_ref[0 : count * SLOTS * LANES, :], we_ref[:, cut], preferred_element_type=F32
            )
            act = scaled_gelu(pre.reshape(count * SLOTS, LANES, 256) + beu_ref[:, cut])
            act = act.reshape(count, SLOTS, LANES, 256)
            if scale is not None:
                act = act * scale
            for at in range(count):
                pos = ring(row + at)
                line = [act[at, slot] for slot in range(SLOTS)]
                line[0], line[-1] = line[0] * edge_left, line[-1] * edge_right
                for pair in range(PAIRS):
                    a, b, c, d = line[2 * pair : 2 * pair + 4]
                    for n, mix in enumerate((a - c, b + c, c - b, b - d)):
                        e_ref[pos, n * PAIRS + pair, :, cut] = mix

    def outer_row(ref, beyond, row, inside):
        fill(0, row, ref[0], beyond)
        gather(0, None)
        expand(1, row, jnp.where(inside, one, nil) if beyond else None)

    def expand_block():
        for at in range(BLOCK):
            row = start + k * BLOCK + at
            fill(at, row, coded_ref[at], False)
            gather(at, row)
        expand(BLOCK, start + k * BLOCK, None)

    def depth_block():
        above = start + (k - 1) * BLOCK
        for part in range(width // 128):
            cut = slice(part * 128, part * 128 + 128)
            taps = [taps_ref[n, :, cut] for n in range(12)]
            for at in range(BLOCK):
                sums = [None, bdu_ref[:, cut], None, None]
                for dy in range(3):
                    pos = ring(above + at + dy - 1)
                    for n in range(4):
                        term = e_ref[pos, n * PAIRS : (n + 1) * PAIRS, :, cut] * taps[4 * dy + n]
                        sums[n] = term if sums[n] is None else sums[n] + term
                act = scaled_gelu(
                    jnp.stack([sums[0] + sums[1] + sums[2], sums[1] - sums[2] - sums[3]], axis=1)
                )
                dp_ref[at * cols : (at + 1) * cols, cut] = act.reshape(cols, 128).astype(BF)
        proj = jnp.dot(dp_ref[...], wp_ref[...], preferred_element_type=F32)
        proj = proj * (0.5 / U) + bp_ref[...]
        for at in range(BLOCK):
            home = xk_ref[lax.rem(above + at, 2 * BLOCK)].astype(F32)
            mixed = home + proj[at * cols : (at + 1) * cols]
            for half, lanes in enumerate(halves):
                for slot in range(STEP):
                    line_ref[at, half, pl.ds(slot, LANES, stride=STEP), :] = mixed[
                        slot * LANES : slot * LANES + LANES, lanes
                    ]
                out_ref[at, :, lanes] = line_ref[at, half].astype(BF)

    for number, (top, bottom) in enumerate(outer):

        @pl.when((segment == number) & (k == 0))
        def _(number=number, top=top):
            outer_row(top, outside[number][0], start - 1, gy > 0)

        @pl.when((segment == number) & (k == last))
        def _(number=number, bottom=bottom):
            outer_row(bottom, outside[number][1], start + last * BLOCK, gy < tall_devs - 1)

    @pl.when(k == 0)
    def _():
        expand_block()

    @pl.when((k > 0) & (k < last))
    def _():
        expand_block()
        depth_block()

    @pl.when(k == last)
    def _():
        depth_block()


def mb_call(coded, scales, rows_beyond, left, right, we, be, dk, bd, wp, bp, firsts, count):
    rows, cols, chans = coded.shape
    width = we.shape[1]
    blocks, segments = count // BLOCK, len(firsts)
    stride = firsts[1] - firsts[0] if segments > 1 else 0
    line = (1, cols, chans)

    def whole(array):
        return pl.BlockSpec(array.shape, lambda i, n=array.ndim: (0,) * n)

    def place(i):
        return i // (blocks + 1), lax.rem(i, blocks + 1)

    def ahead(i):
        segment, k = place(i)
        return (firsts[0] + segment * stride) // BLOCK + jnp.minimum(k, blocks - 1)

    def behind(i):
        segment, k = place(i)
        return segment * blocks + jnp.maximum(k - 1, 0)

    arrays, specs, outside = [], [], []
    for first in firsts:
        outside.append((first == 0, first + count == rows))
        for side, row in enumerate((first - 1, first + count)):
            if outside[-1][side]:
                arrays.append(rows_beyond[side][None])
                specs.append(whole(arrays[-1]))
            else:
                arrays.append(coded)
                specs.append(pl.BlockSpec(line, lambda i, row=row: (row, 0, 0)))
    weights = (we, be, dk, bd, wp, bp)
    cells = count * segments * cols
    return pl.pallas_call(
        functools.partial(mb_kernel, (segments, firsts[0], stride, tuple(outside))),
        grid=(segments * (blocks + 1),),
        out_shape=jax.ShapeDtypeStruct((segments * count, cols, chans), BF),
        in_specs=[
            pl.BlockSpec((BLOCK, cols, chans), lambda i: (ahead(i), 0, 0)),
            whole(scales),
            whole(left),
            whole(right),
            *specs,
            *[whole(a) for a in weights],
        ],
        out_specs=pl.BlockSpec((BLOCK, cols, chans), lambda i: (behind(i), 0, 0)),
        scratch_shapes=[
            pltpu.VMEM((BLOCK, 2, PAD, 128), F32),
            pltpu.VMEM((BLOCK * SLOTS * LANES, chans), BF),
            pltpu.VMEM((RING, 4 * PAIRS, LANES, width), F32),
            pltpu.VMEM((2 * BLOCK, cols, chans), BF),
            pltpu.VMEM((BLOCK * cols, width), BF),
            pltpu.VMEM((12, 8, width), F32),
            pltpu.VMEM((8, width), F32),
            pltpu.VMEM((8, width), F32),
            pltpu.VMEM((2, 2, rows, 128), F32),
            pltpu.VMEM((2, 16 * rows // TILE, 128), F32),
            pltpu.VMEM((BLOCK, 2, cols, 128), F32),
        ],
        compiler_params=pltpu.CompilerParams(
            vmem_limit_bytes=VMEM if segments == 1 else VMEM - 4 * 1024 * 1024
        ),
        cost_estimate=pl.CostEstimate(
            flops=4 * cells * chans * width,
            bytes_accessed=4 * cells * chans,
            transcendentals=2 * cells * width,
        ),
    )(coded, scales, left, right, *arrays, *weights)


def attend_kernel(
    m_ref,
    wq_ref,
    wk_ref,
    wv_ref,
    wo_ref,
    kmask_ref,
    vmask_ref,
    ones_ref,
    out_ref,
    n_ref,
    q_ref,
    k_ref,
    v_ref,
    p_ref,
    a_ref,
    u_ref,
):
    cells, count, chans = m_ref.shape
    total = cells * count
    pairs = HEADS // 2
    m = m_ref[...].astype(F32).reshape(total, chans)
    center = jnp.mean(m, axis=-1, keepdims=True)
    apart = m - center
    spread = jnp.mean(apart * apart, axis=-1, keepdims=True)
    normed = apart * lax.rsqrt(spread + 1e-05)
    for half in range(2):
        n_ref[half] = normed[:, half * 128 : half * 128 + 128]
    qscale = float(HEAD_DIM**-0.5 * 1.4426950408889634)
    tall = jnp.concatenate(
        [
            jnp.concatenate(
                [n_ref[half, pl.ds(g, cells, stride=count), :] for half in range(2)], axis=1
            )
            for g in range(count)
        ],
        axis=0,
    ).astype(BF)
    q_ref[...] = (jnp.dot(tall, wq_ref[...], preferred_element_type=F32) * qscale).astype(BF)
    k_ref[...] = jnp.dot(tall, wk_ref[...], preferred_element_type=F32).astype(BF)
    v_ref[...] = jnp.dot(tall, wv_ref[...], preferred_element_type=F32).astype(BF)

    blank = jnp.zeros((64, 128), BF)
    tall = []
    for g in range(count):
        here = slice(g * cells, (g + 1) * cells)
        k = k_ref[here, :]
        kt = jnp.concatenate([k, k], axis=0).T * kmask_ref[...]
        q = q_ref[here, :]
        parts = []
        for side in range(2):
            lanes = slice(side * 128, side * 128 + 128)
            upper, lower = kt[side * 128 : side * 128 + 64], kt[side * 128 + 64 : side * 128 + 128]
            keys = jnp.concatenate(
                [
                    jnp.concatenate([upper, blank], axis=0),
                    jnp.concatenate([blank, lower], axis=0),
                ],
                axis=1,
            )
            parts.append(jnp.dot(q[:, lanes], keys, preferred_element_type=F32))
        tall.append(jnp.concatenate(parts, axis=1))
    scores = jnp.concatenate(tall, axis=0)
    first = lax.broadcasted_iota(jnp.int32, (1, 128), 1) < 64
    low = jnp.float32(-jnp.inf)
    for pair in range(pairs):
        lanes = slice(pair * 128, pair * 128 + 128)
        two = scores[:, lanes]
        top = jnp.where(
            first,
            jnp.max(jnp.where(first, two, low), axis=-1, keepdims=True),
            jnp.max(jnp.where(first, low, two), axis=-1, keepdims=True),
        )
        p_ref[:, lanes] = jnp.exp2(two - top).astype(BF)
    for g in range(count):
        here = slice(g * cells, (g + 1) * cells)
        for side in range(2):
            lanes = slice(side * 128, side * 128 + 128)
            v = v_ref[here, lanes]
            values = jnp.concatenate(
                [v * vmask_ref[h, :, lanes] for h in range(4 * side, 4 * side + 4)], axis=0
            )
            a_ref[here, lanes] = jnp.dot(
                p_ref[here, side * 256 : side * 256 + 256], values, preferred_element_type=F32
            )
    under = jnp.dot(p_ref[...], ones_ref[...], preferred_element_type=F32)
    attended = (a_ref[...] / under).astype(BF)
    update = jnp.dot(attended, wo_ref[...], preferred_element_type=F32)
    for g in range(count):
        for half in range(2):
            u_ref[half, pl.ds(g, cells, stride=count), :] = update[
                g * cells : (g + 1) * cells, half * 128 : half * 128 + 128
            ]
    for half in range(2):
        out_ref[:, :, half * 128 : half * 128 + 128] = (
            u_ref[half].astype(BF).reshape(cells, count, 128)
        )


def attend_call(moved, wq, wk, wv, wo):
    cells, groups, chans = moved.shape
    count = 16
    total = cells * count
    chan, lane = np.arange(chans), np.arange(128)
    kmask = ((chan[:, None] // HEAD_DIM) % 2 == lane[None, :] // 64).astype(BF)
    head = np.arange(HEADS)
    vmask = np.broadcast_to(
        chan[None, None, :] // HEAD_DIM == head[:, None, None], (HEADS, cells, chans)
    ).astype(BF)
    ones = (chan[None, :] // HEAD_DIM == np.arange(HEADS * cells)[:, None] // cells).astype(BF)

    def whole(array):
        return pl.BlockSpec(array.shape, lambda i, n=array.ndim: (0,) * n)

    return pl.pallas_call(
        attend_kernel,
        grid=(groups // count,),
        out_shape=jax.ShapeDtypeStruct(moved.shape, BF),
        in_specs=[
            pl.BlockSpec((cells, count, chans), lambda i: (0, i, 0)),
            *[whole(a) for a in (wq, wk, wv, wo, kmask, vmask, ones)],
        ],
        out_specs=pl.BlockSpec((cells, count, chans), lambda i: (0, i, 0)),
        scratch_shapes=[
            pltpu.VMEM((2, total, 128), F32),
            pltpu.VMEM((total, chans), BF),
            pltpu.VMEM((total, chans), BF),
            pltpu.VMEM((total, chans), BF),
            pltpu.VMEM((total, HEADS * cells), BF),
            pltpu.VMEM((total, chans), F32),
            pltpu.VMEM((2, total, 128), F32),
        ],
        compiler_params=pltpu.CompilerParams(vmem_limit_bytes=VMEM),
        cost_estimate=pl.CostEstimate(
            flops=2 * cells * groups * chans * (4 * chans + 4 * cells),
            bytes_accessed=4 * cells * groups * chans,
            transcendentals=cells * groups * cells * HEADS,
        ),
    )(moved, wq, wk, wv, wo, kmask, vmask, ones)


def finish_kernel(mixed_ref, home_ref, *refs):
    refs[-1][...] = (mixed_ref[...].astype(F32) + home_ref[...].astype(F32)).astype(BF)


def finish_call(mixed, home, rows, firsts, out):
    block = 16
    blocks = mixed.shape[0] // len(firsts) // block
    stride = (firsts[-1] - firsts[0]) // block
    spec = pl.BlockSpec((block, *mixed.shape[1:]), lambda i: (i, 0, 0))

    def place(i):
        return firsts[0] // block + i // blocks * stride + lax.rem(i, blocks), 0, 0

    held = [] if out is None else [out]
    return pl.pallas_call(
        finish_kernel,
        grid=(mixed.shape[0] // block,),
        out_shape=jax.ShapeDtypeStruct((rows, *mixed.shape[1:]), BF),
        in_specs=[spec, spec, *[pl.BlockSpec(memory_space=pl.ANY) for _ in held]],
        out_specs=pl.BlockSpec(spec.block_shape, place),
        input_output_aliases={2: 0} if held else {},
        compiler_params=pltpu.CompilerParams(vmem_limit_bytes=VMEM),
        cost_estimate=pl.CostEstimate(
            flops=mixed.size, bytes_accessed=6 * mixed.size, transcendentals=0
        ),
    )(mixed, home, *held)


def dequant(line, scales):
    wide = line.astype(F32).reshape(-1, TILE, line.shape[-1]) * scales[:, None, :]
    return wide.astype(BF).reshape(line.shape)


def swap(axis, low, high):
    peers = lax.axis_size(axis)
    up = [(i, i + 1) for i in range(peers - 1)]
    down = [(i + 1, i) for i in range(peers - 1)]
    return lax.ppermute(high, axis, up), lax.ppermute(low, axis, down)


def per_device(
    coded,
    tile_scales,
    expand_weight,
    expand_bias,
    depth_kernel,
    depth_bias,
    project_weight,
    project_bias,
    query_weight,
    key_weight,
    value_weight,
    out_weight,
):
    rows, cols, chans = coded.shape
    first, last = (dequant(coded[:, at], tile_scales[:, at]) for at in (0, -1))
    left, right = swap("gx", first, last)

    def edge(at):
        line = dequant(coded[at], tile_scales[at])
        return jnp.concatenate([left[at][None], line, right[at][None]], axis=0)

    beyond = swap("gy", edge(0), edge(-1))
    wide = lax.axis_size("gx")
    peers = lax.axis_size("gy") * wide
    parity = [[d for d in range(peers) if d % 2 == core] for core in range(2)]

    def exchange(array):
        return lax.all_to_all(array, ("gy", "gx"), 0, 0, tiled=True, axis_index_groups=parity)

    share = (peers // 2, cols * rows // peers, chans)
    parts = [((rows // 4,), rows // 2), ((0, rows * 3 // 4), rows // 4)]
    out = None
    for firsts, count in parts:
        mixed = mb_call(
            coded,
            tile_scales.transpose(1, 0, 2),
            beyond,
            left,
            right,
            expand_weight,
            expand_bias[None, :],
            depth_kernel,
            depth_bias[None, :],
            project_weight,
            project_bias[None, :],
            firsts,
            count,
        )
        if out is None:
            mixed, beyond = lax.optimization_barrier((mixed, beyond))
        moved = exchange(mixed.reshape(share))
        update = attend_call(moved, query_weight, key_weight, value_weight, out_weight)
        home = exchange(update).reshape(mixed.shape)
        out = finish_call(mixed, home, rows, firsts, out)
    return out


def solution(mesh):
    return jax.shard_map(
        per_device,
        mesh=mesh,
        in_specs=(P("gy", "gx", None), P("gy", "gx", None), *[P()] * 10),
        out_specs=P("gy", "gx", None),
        check_vma=False,
    )
```
